128 devices in a mesh: fsdp: 4 (over y_lo, core), ctx: 32 (over z, x, y_hi).
Axes of the slice: x: 4, y: 4 (y_hi: 2, y_lo: 2; y = y_hi * 2 + y_lo), z: 4, core: 2. Of those that a mesh axis runs over, the one named last changes fastest.
Arguments:
- tokens: bfloat16 [4, 8192, 8192], P('fsdp', 'ctx'), may hold values from -6 to 6
- projection: bfloat16 [8192, 1536], P(('fsdp', 'ctx')), may hold values from -0.0625 to 0.0625
- short_taps: float32 [3, 1536], replicated, may hold values from -3 to 3
- long_filters: float32 [32, 8192], P('ctx'), may hold values from -4 to 4
- cotangent: bfloat16 [4, 512, 8192], P('fsdp', None, 'ctx'), may hold values from -6 to 6
Outputs:
- gated: bfloat16 [4, 512, 8192], P('fsdp', None, 'ctx')
- token_grad: bfloat16 [4, 8192, 8192], P('fsdp', 'ctx')
- filter_grad: float32 [32, 8192], P('ctx')
The draws below stay inside these ranges and needn't reach their ends.
All inputs are finite; a program needn't handle non-finite values.
Results may differ from the reference program's by a relative error of at most 0.015.
Values may be sent and summed in bfloat16 or wider, within the bound.
A program may use at most 128 MiB of HBM per device.

```python
import math
import jax
import jax.numpy as jnp
from jax import lax

D = 8192
GSIZE = 16
SEQS = 4
LEN = 8192
C = 512
GROUPS = 32


def draw_long_filters(key, part):
    key = jax.random.fold_in(key, 11)
    key_slow, key_rate, key_noise, key_fast = jax.random.split(key, 4)
    steps_axis = jnp.arange(LEN, dtype=jnp.float32)[None, :]
    slow_share = 0.5
    noise = jnp.clip(jax.random.normal(key_noise, (GROUPS, LEN), jnp.float32), -4.0, 4.0)
    slow = jax.random.bernoulli(key_slow, slow_share, (GROUPS, 1))
    slow_rate = jax.random.uniform(key_rate, (GROUPS, 1), jnp.float32, 0.2, 2.0) / LEN
    fast_rate = jax.random.uniform(key_fast, (GROUPS, 1), jnp.float32, 1.0 / 50.0, 1.0 / 30.0)
    rate = jnp.where(slow, slow_rate, fast_rate)
    envelope = jnp.exp(-rate * steps_axis)
    energy = (1.0 - jnp.exp(-2.0 * rate * LEN)) / (1.0 - jnp.exp(-2.0 * rate))
    return (noise * envelope / jnp.sqrt(energy)).astype(jnp.float32)


def shard_levels(own_key, shape, cuts, low, high):
    def one(dim, shards_of):
        steps = jax.random.uniform(jax.random.fold_in(jax.random.fold_in(own_key, 6), dim), (shards_of,), jnp.float32, low / len(cuts), high / len(cuts))
        return jnp.repeat(jnp.exp(steps), shape[dim] // shards_of).reshape((-1,) + (1,) * (len(shape) - dim - 1))

    gain = one(*cuts[0])
    for cut in cuts[1:]:
        gain = gain * one(*cut)
    return gain


def scatter_about(own_key, dims, spread, reach, shards=(), kind=jnp.bfloat16):
    gain = shard_levels(own_key, dims, shards, -0.22, 0.18) if shards else 1.0
    values = jax.random.normal(own_key, dims, jnp.float32) * spread * gain
    return jnp.minimum(jnp.maximum(values, -reach), reach).astype(kind)


def setup_inputs(seed: int = 0) -> dict:
    seeds = jax.random.split(jax.random.key(seed), 6)
    tokens = scatter_about(seeds[0], (SEQS, LEN, D), 1.0, 6.0, ((0, 4), (1, 32)))
    projection = scatter_about(seeds[1], (D, 3 * C), D ** -0.5, 0.0625, ((0, 128),))
    short_taps = scatter_about(seeds[2], (3, 3 * C), 0.6, 3.0, (), jnp.float32)
    long_filters = draw_long_filters(jax.random.fold_in(seeds[5], 71), 0)
    cotangent = scatter_about(seeds[4], (SEQS, C, LEN), 1.0, 6.0, ((0, 4), (2, 32)))
    return dict(tokens=tokens, projection=projection, short_taps=short_taps, long_filters=long_filters, cotangent=cotangent)


def short_forward(values, tap):
    length = values.shape[2]
    padded = jnp.pad(values, ((0, 0), (0, 0), (2, 0)))
    return tap[0][:, :, None] * values + tap[1][:, :, None] * padded[:, :, 1:length + 1] + tap[2][:, :, None] * padded[:, :, 0:length]

def short_backward(values, tap):
    length = values.shape[2]
    padded = jnp.pad(values, ((0, 0), (0, 0), (0, 2)))
    return tap[0][:, :, None] * values + tap[1][:, :, None] * padded[:, :, 1:length + 1] + tap[2][:, :, None] * padded[:, :, 2:length + 2]

def reference(tokens, projection, short_taps, long_filters, cotangent):
    channels = projection.shape[1] // 3
    length = tokens.shape[1]
    total = 2 * length
    tap = short_taps.reshape(3, 3, channels)
    filter_spec = jnp.repeat(jnp.fft.rfft(long_filters, n=total, axis=1), GSIZE, axis=0)

    def one_sequence(pair):
        rows, upstream = pair
        proj = jnp.dot(rows, projection, preferred_element_type=jnp.float32).astype(jnp.bfloat16)
        proj = proj.T.reshape(3, channels, length).astype(jnp.float32)
        parts = short_forward(proj, tap)
        query, key_part, value = (parts[0], parts[1], parts[2])
        mixed = (key_part * value).astype(jnp.bfloat16)
        mixed_spec = jnp.fft.rfft(mixed.astype(jnp.float32), n=total, axis=1)
        conv = jnp.fft.irfft(mixed_spec * filter_spec, n=total, axis=1)[:, :length].astype(jnp.bfloat16)
        conv_wide = conv.astype(jnp.float32)
        gated = (query * conv_wide).astype(jnp.bfloat16)
        upstream = upstream.astype(jnp.float32)
        gate_grad = (upstream * query).astype(jnp.bfloat16)
        query_grad = upstream * conv_wide
        grad_spec = jnp.fft.rfft(gate_grad.astype(jnp.float32), n=total, axis=1)
        mixed_grad = jnp.fft.irfft(grad_spec * jnp.conj(filter_spec), n=total, axis=1)[:, :length].astype(jnp.bfloat16)
        cross = jnp.fft.irfft(grad_spec * jnp.conj(mixed_spec), n=total, axis=1)[:, :length]
        filter_part = cross.reshape(GROUPS, GSIZE, length).sum(axis=1)
        mixed_wide = mixed_grad.astype(jnp.float32)
        grads = jnp.stack([query_grad, mixed_wide * value, mixed_wide * key_part])
        proj_grad = short_backward(grads, tap).astype(jnp.bfloat16).reshape(3 * channels, length)
        token_grad = jnp.dot(proj_grad.T, projection.T, preferred_element_type=jnp.float32).astype(jnp.bfloat16)
        return (gated, token_grad, filter_part)
    gated, token_grad, filter_parts = lax.map(one_sequence, (tokens, cotangent))
    filter_grad = lax.optimization_barrier(jnp.sum(filter_parts, axis=0)) * (1.0 / math.sqrt(SEQS * GSIZE * LEN))
    return (gated, token_grad, filter_grad)
```

```python
import functools
import math

import jax
import jax.numpy as jnp
from jax import lax
from jax.experimental import pallas as pl
from jax.experimental.pallas import tpu as pltpu
from jax.sharding import PartitionSpec as P

MESH = pl.DeviceIdType.MESH
BF = jnp.bfloat16
F32 = jnp.float32
FULL = slice(None)
ORDERS = ((0, 1, 2), (1, 2, 0), (2, 0, 1))


def my_coords():
    f = lax.axis_index("fsdp")
    t = lax.axis_index("ctx")
    return f % 2, (t // 8, (t // 2) % 4, (t % 2) * 2 + f // 2)


def device_of(core, pos):
    z, x, y = pos
    return ((y % 2) * 2 + core, z * 8 + x * 2 + y // 2)


def moved(pos, axis, by):
    out = list(pos)
    out[axis] = (pos[axis] + by) % 4
    return tuple(out)


def shards(ref, part, core, pos, half=None):
    z, x, y = pos
    rows = FULL if half is None else pl.ds(half * 32, 32)
    yl = FULL if y is None else y % 2
    yh = FULL if y is None else y // 2
    z = FULL if z is None else z
    x = FULL if x is None else x
    return ref.at[part, yl, core, z, x, yh, rows, :]


class Gather:
    def __init__(self, w, own, send, recv, sib_send, sib_recv):
        self.w, self.own = w, own
        self.send, self.recv = send, recv
        self.sib_send, self.sib_recv = sib_send, sib_recv
        self.core, self.pos = my_coords()
        self.started = []

    def block(self, part, phase, at, half=None, core=None):
        order = ORDERS[part]
        pos = [None, None, None]
        for later in order[phase + 1 :]:
            pos[later] = self.pos[later]
        pos[order[phase]] = at
        return shards(self.w, part, self.core if core is None else core, pos, half)

    def copy(self, part, phase, kind, at, by, half=None):
        axis = ORDERS[part][phase]
        ref = self.block(part, phase, at, half)
        return pltpu.make_async_remote_copy(
            src_ref=ref,
            dst_ref=ref,
            send_sem=self.send.at[part, phase, kind],
            recv_sem=self.recv.at[part, phase, kind],
            device_id=device_of(self.core, moved(self.pos, axis, by)),
            device_id_type=MESH,
        )

    def go(self, c):
        c.start()
        self.started.append(c)

    def me(self, part, phase):
        return self.pos[ORDERS[part][phase]]

    def first(self, part, phase):
        m = self.me(part, phase)
        self.go(self.copy(part, phase, 0, m, 1))
        self.go(self.copy(part, phase, 1, m, -1))

    def forward(self, part, phase, kind):
        m = self.me(part, phase)
        by = 1 if kind == 0 else -1
        at = (m - by) % 4
        self.copy(part, phase, kind, at, by).wait_recv()
        self.go(self.copy(part, phase, 2 + kind, at, by, half=kind))

    def last(self, part, phase, kind):
        m = self.me(part, phase)
        self.copy(part, phase, 2 + kind, (m + 2) % 4, 1, half=kind).wait_recv()

    def sibling(self, part, kind, at, half=None, receive=False):
        core = 1 - self.core if receive else self.core
        ref = self.block(part, 2, at, half, core)
        return pltpu.make_async_remote_copy(
            src_ref=ref,
            dst_ref=ref,
            send_sem=self.sib_send.at[part, kind],
            recv_sem=self.sib_recv.at[part, kind],
            device_id=device_of(1 - self.core, self.pos),
            device_id_type=MESH,
        )

    def wait_sends(self):
        for c in self.started:
            c.wait_send()


def gather_kernel(own, out, w, put, send, recv, sib_send, sib_recv, out_sem):
    g = Gather(w, own, send, recv, sib_send, sib_recv)
    barrier = pltpu.get_barrier_semaphore()
    for axis in range(3):
        for by in (1, -1):
            pl.semaphore_signal(
                barrier, inc=1, device_id=device_of(g.core, moved(g.pos, axis, by)), device_id_type=MESH
            )
    pl.semaphore_signal(barrier, inc=1, device_id=device_of(1 - g.core, g.pos), device_id_type=MESH)
    mine = []
    for part in range(3):
        c = pltpu.make_async_copy(
            own.at[:, pl.ds(512 * part, 512)], shards(w, part, g.core, g.pos), put.at[part]
        )
        c.start()
        mine.append(c)
    for c in mine:
        c.wait()
    pl.semaphore_wait(barrier, 7)
    for part in range(3):
        g.first(part, 0)
    for phase in range(3):
        for kind in range(2):
            for part in range(3):
                g.forward(part, phase, kind)
                if phase == 2:
                    g.go(g.sibling(part, 1 + kind, (g.me(part, 2) + (-1, 1)[kind]) % 4))
        for part in range(3):
            for kind in range(2):
                g.last(part, phase, kind)
                if phase == 2:
                    g.go(g.sibling(part, 3 + kind, (g.me(part, 2) + 2) % 4, half=kind))
            if phase < 2:
                g.first(part, phase + 1)
            if phase == 1:
                g.go(g.sibling(part, 0, g.me(part, 2)))
    for part in range(3):
        m = g.me(part, 2)
        g.sibling(part, 0, m, receive=True).wait_recv()
        g.sibling(part, 1, (m + 3) % 4, receive=True).wait_recv()
        g.sibling(part, 2, (m + 1) % 4, receive=True).wait_recv()
        for kind in range(2):
            g.sibling(part, 3 + kind, (m + 2) % 4, half=kind, receive=True).wait_recv()
        pltpu.make_async_copy(w.at[part], out.at[part], out_sem.at[part]).start()
    g.wait_sends()
    for part in range(3):
        pltpu.make_async_copy(w.at[part], out.at[part], out_sem.at[part]).wait()


def gather(projection):
    return pl.pallas_call(
        gather_kernel,
        out_shape=jax.ShapeDtypeStruct((3, 2, 2, 4, 4, 2, 64, 512), BF),
        in_specs=[pl.BlockSpec(memory_space=pltpu.VMEM)],
        out_specs=pl.BlockSpec(memory_space=pl.ANY),
        scratch_shapes=[
            pltpu.VMEM((3, 2, 2, 4, 4, 2, 64, 512), BF),
            pltpu.SemaphoreType.DMA((3,)),
            pltpu.SemaphoreType.DMA((3, 3, 4)),
            pltpu.SemaphoreType.DMA((3, 3, 4)),
            pltpu.SemaphoreType.DMA((3, 5)),
            pltpu.SemaphoreType.DMA((3, 5)),
            pltpu.SemaphoreType.DMA((3,)),
        ],
        compiler_params=pltpu.CompilerParams(
            collective_id=0, has_side_effects=True, vmem_limit_bytes=48 * 1024 * 1024
        ),
    )(projection)


HIGHEST = lax.Precision.HIGHEST
THREEPASS = lax.Precision.HIGH


def split_halves(table):
    upper = table.astype(jnp.bfloat16)
    lower = (table - upper.astype(jnp.float32)).astype(jnp.bfloat16)
    return (upper, lower)


def dft_tables(total_len, inner_len):
    outer_len = total_len // inner_len
    halved = outer_len // 2
    outer_rows = jnp.arange(outer_len, dtype=jnp.int32)[:, None]
    lower_cols = jnp.arange(halved, dtype=jnp.int32)[None, :]
    outer_angle = (outer_rows * lower_cols % outer_len).astype(jnp.float32) * (
        2.0 * math.pi / outer_len
    )
    inner_cols = jnp.arange(inner_len, dtype=jnp.int32)[None, :]
    twist_angle = (outer_rows * inner_cols % total_len).astype(jnp.float32) * (
        2.0 * math.pi / total_len
    )
    inner_rows = jnp.arange(inner_len, dtype=jnp.int32)[:, None]
    inner_angle = (inner_rows * inner_cols % inner_len).astype(jnp.float32) * (
        2.0 * math.pi / inner_len
    )
    outer_cos = jnp.cos(outer_angle)
    outer_sin = -jnp.sin(outer_angle)
    return (
        outer_cos,
        outer_sin,
        jnp.cos(twist_angle),
        -jnp.sin(twist_angle),
        jnp.cos(inner_angle),
        -jnp.sin(inner_angle),
        split_halves(outer_cos),
        split_halves(outer_sin),
    )


def first_section(table, halves, blocks):
    if blocks.dtype == jnp.bfloat16:
        upper, lower = halves
        return jnp.einsum(
            "ka,cab->ckb", upper, blocks, preferred_element_type=jnp.float32
        ) + jnp.einsum("ka,cab->ckb", lower, blocks, preferred_element_type=jnp.float32)
    return jnp.einsum("ka,cab->ckb", table, blocks, precision=HIGHEST)


def forward_spectrum(signal, tables):
    outer_cos, outer_sin, twist_cos, twist_sin, inner_cos, inner_sin, cos_halves, sin_halves = (
        tables
    )
    blocks = signal.reshape(signal.shape[0], -1, inner_cos.shape[0])
    real_part = first_section(outer_cos, cos_halves, blocks)
    imag_part = first_section(outer_sin, sin_halves, blocks)
    turned_real = real_part * twist_cos - imag_part * twist_sin
    turned_imag = real_part * twist_sin + imag_part * twist_cos
    spec_real = jnp.einsum("ckb,bm->ckm", turned_real, inner_cos, precision=THREEPASS) - jnp.einsum(
        "ckb,bm->ckm", turned_imag, inner_sin, precision=THREEPASS
    )
    spec_imag = jnp.einsum("ckb,bm->ckm", turned_real, inner_sin, precision=THREEPASS) + jnp.einsum(
        "ckb,bm->ckm", turned_imag, inner_cos, precision=THREEPASS
    )
    return (spec_real, spec_imag)


def inverse_signal(spec_real, spec_imag, tables):
    outer_cos, outer_sin, twist_cos, twist_sin, inner_cos, inner_sin, cos_halves, sin_halves = (
        tables
    )
    total_len = outer_cos.shape[0] * inner_cos.shape[0]
    back_real = jnp.einsum("ckm,mb->ckb", spec_real, inner_cos, precision=THREEPASS) + jnp.einsum(
        "ckm,mb->ckb", spec_imag, inner_sin, precision=THREEPASS
    )
    back_imag = jnp.einsum("ckm,mb->ckb", spec_imag, inner_cos, precision=THREEPASS) - jnp.einsum(
        "ckm,mb->ckb", spec_real, inner_sin, precision=THREEPASS
    )
    turned_real = back_real * twist_cos + back_imag * twist_sin
    turned_imag = back_imag * twist_cos - back_real * twist_sin
    signal = jnp.einsum("ka,ckb->cab", outer_cos, turned_real, precision=THREEPASS) + jnp.einsum(
        "ka,ckb->cab", outer_sin, turned_imag, precision=THREEPASS
    )
    return signal.reshape(signal.shape[0], -1) * (1.0 / total_len)


def long_forward(mixed, long_filters, tables):
    groups = long_filters.shape[0]
    filt_real, filt_imag = forward_spectrum(long_filters, tables)
    mix_real, mix_imag = forward_spectrum(mixed, tables)
    grouped = (groups, -1) + mix_real.shape[1:]
    split_real = mix_real.reshape(grouped)
    split_imag = mix_imag.reshape(grouped)
    prod_real = split_real * filt_real[:, None] - split_imag * filt_imag[:, None]
    prod_imag = split_real * filt_imag[:, None] + split_imag * filt_real[:, None]
    conv = inverse_signal(
        prod_real.reshape(mix_real.shape), prod_imag.reshape(mix_real.shape), tables
    )
    return (conv.astype(jnp.bfloat16), (split_real, split_imag, filt_real, filt_imag))


def long_backward(gate_grad, saved, tables):
    split_real, split_imag, filt_real, filt_imag = saved
    grad_real, grad_imag = forward_spectrum(gate_grad, tables)
    grad_split_real = grad_real.reshape(split_real.shape)
    grad_split_imag = grad_imag.reshape(split_real.shape)
    back_real = grad_split_real * filt_real[:, None] + grad_split_imag * filt_imag[:, None]
    back_imag = grad_split_imag * filt_real[:, None] - grad_split_real * filt_imag[:, None]
    mixed_grad = inverse_signal(
        back_real.reshape(grad_real.shape), back_imag.reshape(grad_real.shape), tables
    )
    cross_real = jnp.sum(grad_split_real * split_real + grad_split_imag * split_imag, axis=1)
    cross_imag = jnp.sum(grad_split_imag * split_real - grad_split_real * split_imag, axis=1)
    filter_part = inverse_signal(cross_real, cross_imag, tables)
    return (mixed_grad.astype(jnp.bfloat16), filter_part)


def short_forward(values, tap, before):
    length = values.shape[2]
    extended = jnp.concatenate([before, values], axis=2)
    return (
        tap[0][:, :, None] * values
        + tap[1][:, :, None] * extended[:, :, 1 : length + 1]
        + tap[2][:, :, None] * extended[:, :, 0:length]
    )


def short_backward(values, tap, after):
    length = values.shape[2]
    extended = jnp.concatenate([values, after], axis=2)
    return (
        tap[0][:, :, None] * values
        + tap[1][:, :, None] * extended[:, :, 1 : length + 1]
        + tap[2][:, :, None] * extended[:, :, 2 : length + 2]
    )


def body(tokens, projection, short_taps, long_filters, cotangent):
    rows = tokens.shape[1]
    columns = projection.shape[1]
    channels = columns // 3
    context = lax.axis_size("ctx")
    local_channels = channels // context
    length = rows * context
    group_size = local_channels // long_filters.shape[0]
    tables = dft_tables(2 * length, math.gcd(rows, 128))
    tap_all = short_taps.reshape(3, 3, channels)
    weights = gather(projection).reshape(3, tokens.shape[2], channels)
    proj = jnp.einsum("td,pdc->pct", tokens[0], weights, preferred_element_type=jnp.float32)
    proj = proj.astype(jnp.bfloat16)
    upstream = cotangent[0]
    moved = lax.all_to_all(proj, "ctx", split_axis=1, concat_axis=2, tiled=True)
    start = lax.axis_index("ctx") * local_channels
    tap_mine = lax.dynamic_slice_in_dim(tap_all, start, local_channels, 2)
    values = moved.astype(jnp.float32)
    parts = short_forward(values, tap_mine, jnp.zeros_like(values[:, :, :2]))
    query, key_part, value = (parts[0], parts[1], parts[2])
    mixed = (key_part * value).astype(jnp.bfloat16)
    conv, saved = long_forward(mixed, long_filters, tables)
    conv_wide = conv.astype(jnp.float32)
    gated_local = (query * conv_wide).astype(jnp.bfloat16)
    gated = lax.all_to_all(gated_local, "ctx", split_axis=1, concat_axis=0, tiled=True)
    arriving = lax.all_to_all(upstream, "ctx", split_axis=0, concat_axis=1, tiled=True).astype(
        jnp.float32
    )
    gate_grad = (arriving * query).astype(jnp.bfloat16)
    query_grad = arriving * conv_wide
    mixed_grad, filter_part = long_backward(gate_grad, saved, tables)
    mixed_wide = mixed_grad.astype(jnp.float32)
    grads = jnp.stack([query_grad, mixed_wide * value, mixed_wide * key_part])
    local_grad = short_backward(grads, tap_mine, jnp.zeros_like(grads[:, :, :2])).astype(
        jnp.bfloat16
    )
    proj_grad = lax.all_to_all(local_grad, "ctx", split_axis=2, concat_axis=1, tiled=True)
    scale = 1.0 / math.sqrt(lax.axis_size("fsdp") * group_size * length)
    filter_grad = lax.psum(filter_part.astype(jnp.bfloat16), "fsdp").astype(jnp.float32) * scale
    token_grad = jnp.einsum(
        "pct,pdc->td", proj_grad.reshape(3, channels, rows), weights, preferred_element_type=jnp.float32
    ).astype(jnp.bfloat16)
    return (gated[None], token_grad[None], filter_grad)


def solution(mesh):
    in_specs = (
        P("fsdp", "ctx", None),
        P(("fsdp", "ctx"), None),
        P(),
        P("ctx", None),
        P("fsdp", None, "ctx"),
    )
    out_specs = (P("fsdp", None, "ctx"), P("fsdp", "ctx", None), P("ctx", None))
    return jax.shard_map(body, mesh=mesh, in_specs=in_specs, out_specs=out_specs, check_vma=False)
```

```python
import math

import jax
import jax.numpy as jnp
from jax import lax
from jax.experimental import pallas as pl
from jax.experimental.pallas import tpu as pltpu
from jax.sharding import PartitionSpec as P

MESH = pl.DeviceIdType.MESH
BF = jnp.bfloat16
F32 = jnp.float32
FULL = slice(None)
ORDERS = ((0, 1, 2), (1, 2, 0), (2, 0, 1))


def my_coords():
    f = lax.axis_index("fsdp")
    t = lax.axis_index("ctx")
    return f % 2, (t // 8, (t // 2) % 4, (t % 2) * 2 + f // 2)


def device_of(core, pos):
    z, x, y = pos
    return ((y % 2) * 2 + core, z * 8 + x * 2 + y // 2)


def moved(pos, axis, by):
    out = list(pos)
    out[axis] = (pos[axis] + by) % 4
    return tuple(out)


def shards(ref, part, core, pos, half=None):
    z, x, y = pos
    rows = FULL if half is None else pl.ds(half * 32, 32)
    yl = FULL if y is None else y % 2
    yh = FULL if y is None else y // 2
    z = FULL if z is None else z
    x = FULL if x is None else x
    return ref.at[part, yl, core, z, x, yh, rows, :]


class Gather:
    def __init__(self, w, own, send, recv, sib_send, sib_recv):
        self.w, self.own = w, own
        self.send, self.recv = send, recv
        self.sib_send, self.sib_recv = sib_send, sib_recv
        self.core, self.pos = my_coords()
        self.started = []

    def block(self, part, phase, at, half=None, core=None):
        order = ORDERS[part]
        pos = [None, None, None]
        for later in order[phase + 1 :]:
            pos[later] = self.pos[later]
        pos[order[phase]] = at
        return shards(self.w, part, self.core if core is None else core, pos, half)

    def copy(self, part, phase, kind, at, by, half=None):
        axis = ORDERS[part][phase]
        ref = self.block(part, phase, at, half)
        return pltpu.make_async_remote_copy(
            src_ref=ref,
            dst_ref=ref,
            send_sem=self.send.at[part, phase, kind],
            recv_sem=self.recv.at[part, phase, kind],
            device_id=device_of(self.core, moved(self.pos, axis, by)),
            device_id_type=MESH,
        )

    def go(self, c):
        c.start()
        self.started.append(c)

    def me(self, part, phase):
        return self.pos[ORDERS[part][phase]]

    def first(self, part, phase):
        m = self.me(part, phase)
        self.go(self.copy(part, phase, 0, m, 1))
        self.go(self.copy(part, phase, 1, m, -1))

    def forward(self, part, phase, kind):
        m = self.me(part, phase)
        by = 1 if kind == 0 else -1
        at = (m - by) % 4
        self.copy(part, phase, kind, at, by).wait_recv()
        self.go(self.copy(part, phase, 2 + kind, at, by, half=kind))

    def last(self, part, phase, kind):
        m = self.me(part, phase)
        self.copy(part, phase, 2 + kind, (m + 2) % 4, 1, half=kind).wait_recv()

    def sibling(self, part, kind, at, half=None, receive=False):
        core = 1 - self.core if receive else self.core
        ref = self.block(part, 2, at, half, core)
        return pltpu.make_async_remote_copy(
            src_ref=ref,
            dst_ref=ref,
            send_sem=self.sib_send.at[part, kind],
            recv_sem=self.sib_recv.at[part, kind],
            device_id=device_of(1 - self.core, self.pos),
            device_id_type=MESH,
        )

    def wait_sends(self):
        for c in self.started:
            c.wait_send()


DN_NT = (((1,), (1,)), ((), ()))
KK = 4


def lanes(shape):
    return lax.broadcasted_iota(jnp.int32, shape, len(shape) - 1)


def fill_toeplitz(h_ref, s_ref):
    @pl.loop(0, 32)
    def _(k):
        now = h_ref[:, pl.ds(pl.multiple_of(256 * k, 256), 256)]
        earlier = jnp.maximum(k - 1, 0)
        before = h_ref[:, pl.ds(pl.multiple_of(256 * earlier, 256), 256)]
        before = jnp.where(k > 0, before, 0.0)
        row = jnp.concatenate([before, now], axis=1)
        base = pltpu.roll(jnp.broadcast_to(row, (8, 512)), 0, 1, stride=1, stride_axis=0)
        for b in range(8):
            one = base if b == 0 else pltpu.roll(base, 16 * b, 1)
            two = pltpu.roll(base, 16 * b + 8, 1)
            pair = jnp.concatenate([one, two], axis=0).astype(BF)
            s_ref[k, 16 * b : 16 * b + 16, :] = pair[:, 256:512]
            s_ref[k, 128 + 16 * b : 144 + 16 * b, :] = pair[:, 128:384]


def fill_taps(taps_ref, tap_ref, group):
    lane = lanes((16, 512))
    chan = lax.broadcasted_iota(jnp.int32, (16, 512), 0)
    pick = (lane == group * 16 + chan).astype(F32)
    for tap in range(3):
        for part in range(3):
            row = taps_ref[tap : tap + 1, 512 * part : 512 * part + 512]
            col = jnp.sum(pick * row, axis=1, keepdims=True)
            tap_ref[3 * tap + part] = jnp.broadcast_to(col, (16, 256))


def conv_front(x_ref, u_ref, tap_ref, wide_ref, mpad_ref, gpad_ref):
    lane = lanes((16, 256))
    mpad_ref[0:512, :] = jnp.zeros((512, 256), BF)
    gpad_ref[512:1024, :] = jnp.zeros((512, 256), BF)

    @pl.loop(0, 32)
    def _(a):
        prev = jnp.maximum(a - 1, 0)
        got = []
        for part in range(3):
            x = x_ref[part, a].astype(F32)
            y = x_ref[part, prev].astype(F32)
            y = jnp.where(a > 0, y, 0.0)
            one = jnp.where(lane < 1, pltpu.roll(y, 1, 1), pltpu.roll(x, 1, 1))
            two = jnp.where(lane < 2, pltpu.roll(y, 2, 1), pltpu.roll(x, 2, 1))
            short = tap_ref[part] * x + tap_ref[3 + part] * one + tap_ref[6 + part] * two
            wide_ref[part, a] = short
            got.append(short)
        rows = pl.ds(pl.multiple_of(16 * a, 16), 16)
        later = pl.ds(pl.multiple_of(512 + 16 * a, 16), 16)
        mpad_ref[later, :] = (got[1] * got[2]).astype(BF)
        gpad_ref[rows, :] = (u_ref[a].astype(F32) * got[0]).astype(BF)


def long_conv(mpad_ref, s_ref, acc_ref):
    acc_ref[...] = jnp.zeros_like(acc_ref)

    @pl.loop(0, 32 // KK)
    def _(n):
        lhs, rhs = [], []
        for i in range(KK):
            k = n * KK + i
            lhs.append(mpad_ref[pl.ds(pl.multiple_of(512 - 16 * k, 16), 512), :])
            rhs.append(s_ref[k])
        acc_ref[...] += jnp.dot(
            jnp.concatenate(lhs, axis=1), jnp.concatenate(rhs, axis=0), preferred_element_type=F32
        )


def long_back(gpad_ref, s_ref, acc_ref):
    acc_ref[...] = jnp.zeros_like(acc_ref)

    @pl.loop(0, 32 // KK)
    def _(n):
        lhs, rhs = [], []
        for i in range(KK):
            k = n * KK + i
            lhs.append(gpad_ref[pl.ds(pl.multiple_of(16 * k, 16), 512), :])
            rhs.append(s_ref[k])
        acc_ref[...] += lax.dot_general(
            jnp.concatenate(lhs, axis=1),
            jnp.concatenate(rhs, axis=1),
            DN_NT,
            preferred_element_type=F32,
        )


def gate_and_query_grad(acc_ref, u_ref, wide_ref, gated_ref, grad_ref):
    @pl.loop(0, 32)
    def _(a):
        rows = pl.ds(pl.multiple_of(16 * a, 16), 16)
        conv = acc_ref[rows, :].astype(BF).astype(F32)
        gated_ref[a] = (wide_ref[0, a] * conv).astype(BF)
        grad_ref[0, a] = u_ref[a].astype(F32) * conv


def back_taps(part, a, tap_ref, grad_ref, pg_ref):
    lane = lanes((16, 256))
    x = grad_ref[part, a]
    y = grad_ref[part, a + 1]
    one = jnp.where(lane > 254, pltpu.roll(y, 255, 1), pltpu.roll(x, 255, 1))
    two = jnp.where(lane > 253, pltpu.roll(y, 254, 1), pltpu.roll(x, 254, 1))
    out = tap_ref[part] * x + tap_ref[3 + part] * one + tap_ref[6 + part] * two
    pg_ref[part, a] = out.astype(BF)


def query_back(tap_ref, grad_ref, pg_ref):
    grad_ref[:, 32] = jnp.zeros((3, 16, 256), F32)

    @pl.loop(0, 32)
    def _(a):
        back_taps(0, a, tap_ref, grad_ref, pg_ref)


def key_value_back(acc_ref, wide_ref, tap_ref, grad_ref, pg_ref):
    @pl.loop(0, 32)
    def _(n):
        a = 31 - n
        rows = pl.ds(pl.multiple_of(16 * a, 16), 16)
        mg = acc_ref[rows, :].astype(BF).astype(F32)
        grad_ref[1, a] = mg * wide_ref[2, a]
        grad_ref[2, a] = mg * wide_ref[1, a]
        back_taps(1, a, tap_ref, grad_ref, pg_ref)
        back_taps(2, a, tap_ref, grad_ref, pg_ref)


def filter_back(mpad_ref, gpad_ref, mt_ref, z_ref, out_ref, kk=2):
    mt_ref[...] = mpad_ref[512:1024, :].astype(F32).T.astype(BF)
    z_ref[...] = jnp.zeros_like(z_ref)

    @pl.loop(0, 32 // kk)
    def _(n):
        for i in range(kk):
            k = n * kk + i
            q = jnp.dot(
                mt_ref[...],
                gpad_ref[pl.ds(pl.multiple_of(16 * k, 16), 512), :],
                preferred_element_type=F32,
            )
            top, low = q[0:128], q[128:256]
            x = jnp.concatenate(
                [jnp.zeros((128, 128), F32), low[:, 0:128], top[:, 0:128] + low[:, 128:256], top[:, 128:256]],
                axis=1,
            )
            for half in (64, 32, 16, 8):
                x = x[0:half] + pltpu.roll(x[half : 2 * half], 512 - half, 1)
            at = pl.ds(pl.multiple_of(256 * k, 256), 512)
            z_ref[:, at] += x
    x = z_ref[...]
    size = z_ref.shape[1]
    row = lax.broadcasted_iota(jnp.int32, x.shape, 0)
    for bit in (1, 2, 4):
        x = jnp.where(row // bit % 2 == 1, pltpu.roll(x, size - bit, 1), x)
    out_ref[...] = jnp.sum(x[:, 256:], axis=0, keepdims=True)


def each_peer(step):
    @pl.loop(1, 32)
    def _(d):
        step(d)


class Exchange:
    def __init__(self, src, dst, send, recv):
        self.src, self.dst, self.send, self.recv = src, dst, send, recv
        self.f, self.t = lax.axis_index("fsdp"), lax.axis_index("ctx")

    def copy(self, d):
        peer = (self.t + d) % 32
        return pltpu.make_async_remote_copy(
            src_ref=self.src(peer),
            dst_ref=self.dst(self.t),
            send_sem=self.send.at[d],
            recv_sem=self.recv.at[d],
            device_id=(self.f, peer),
            device_id_type=MESH,
        )

    def start(self):
        each_peer(lambda d: self.copy(d).start())

    def wait_recv(self):
        each_peer(lambda d: self.copy(d).wait_recv())

    def wait_send(self):
        each_peer(lambda d: self.copy(d).wait_send())


def project(part, near, pos, tok, w, acc):
    z, x, y = pos
    yl = y % 2

    @pl.loop(0, 8)
    def _(n):
        if part == 0:
            fy, fc, fz = (1 - yl if near else yl), n // 4, n % 4
        elif part == 1:
            fy, fc, fz = n // 4, n // 2 % 2, (z + n % 2 * 2 + near) % 4
        else:
            fy, fc, fz = n // 4, n // 2 % 2, n % 2 * 2
        row = (fy * 2 + fc) * 4 + fz
        if part < 2:
            lhs = tok[:, pl.ds(pl.multiple_of(row * 512, 512), 512)]
            rhs = w[part, fy, fc, fz].reshape(512, 512)
        else:
            left, right = [], []
            for i in range(2):
                for hop in (0, 2):
                    fx = (x + near + hop) % 4
                    at = pl.multiple_of(((row + i) * 4 + fx) * 128, 128)
                    left.append(tok[:, pl.ds(at, 128)])
                    right.append(w[part, fy, fc, fz + i, fx].reshape(128, 512))
            lhs = jnp.concatenate(left, axis=1)
            rhs = jnp.concatenate(right, axis=0)
        acc[part] += jnp.dot(lhs, rhs, preferred_element_type=F32)


def kernel(
    tok_hbm, own, taps, h, cot_hbm,
    gated_out, grad_out, filter_out,
    w, tok, acc3, p, x, u, s, tap, wide, mpad, gpad, acc, grad, pg, r, pgt, mt, z8, total, gated, fmine, fgot,
    put, send, recv, sib_send, sib_recv, local, a2a_send, a2a_recv, f_send, f_recv, out_sem,
):
    g = Gather(w, own, send, recv, sib_send, sib_recv)
    f, t = lax.axis_index("fsdp"), lax.axis_index("ctx")
    core, pos = g.core, g.pos
    barrier = pltpu.get_barrier_semaphore()

    def hello(device):
        pl.semaphore_signal(barrier, inc=1, device_id=device, device_id_type=MESH)

    each_peer(lambda d: hello((f, (t + d) % 32)))
    for d in range(1, 4):
        hello(((f + d) % 4, t))
    hello(((f + 2) % 4, t + 1 - t % 2 * 2))
    load = pltpu.make_async_copy(tok_hbm, tok, local.at[0])
    load.start()
    mine = []
    for part in range(3):
        c = pltpu.make_async_copy(
            own.at[:, pl.ds(512 * part, 512)], shards(w, part, core, pos), put.at[part]
        )
        c.start()
        mine.append(c)
    my_cot = pltpu.make_async_copy(cot_hbm.at[t], u.at[t], local.at[1])
    my_cot.start()
    for c in mine:
        c.wait()
    pl.semaphore_wait(barrier, 35)

    cots = Exchange(lambda q: cot_hbm.at[q], lambda q: u.at[q], a2a_send.at[0], a2a_recv.at[0])
    projs = Exchange(lambda q: p.at[:, q], lambda q: x.at[:, q], a2a_send.at[1], a2a_recv.at[1])
    gates = Exchange(lambda q: gated.at[q], lambda q: gated_out.at[q], a2a_send.at[2], a2a_recv.at[2])
    firsts = Exchange(lambda q: pg.at[0, q], lambda q: r.at[0, q], a2a_send.at[3], a2a_recv.at[3])
    others = Exchange(
        lambda q: pg.at[pl.ds(1, 2), q], lambda q: r.at[pl.ds(1, 2), q], a2a_send.at[4], a2a_recv.at[4]
    )

    for part in range(3):
        g.first(part, 0)
    fill_taps(taps, tap, t)
    acc3[...] = jnp.zeros_like(acc3)
    for phase in range(3):
        if phase == 2:
            cots.start()
            fill_toeplitz(h, s)
            load.wait()
        for kind in range(2):
            for part in range(3):
                g.forward(part, phase, kind)
                if phase == 2:
                    g.go(g.sibling(part, 1 + kind, (g.me(part, 2) + (-1, 1)[kind]) % 4))
        if phase == 2:
            for part in range(3):
                m = g.me(part, 2)
                g.sibling(part, 1, (m + 3) % 4, receive=True).wait_recv()
                g.sibling(part, 2, (m + 1) % 4, receive=True).wait_recv()
                project(part, 1, pos, tok, w, acc3)
        for part in range(3):
            for kind in range(2):
                g.last(part, phase, kind)
                if phase == 2:
                    g.go(g.sibling(part, 3 + kind, (g.me(part, 2) + 2) % 4, half=kind))
            if phase < 2:
                g.first(part, phase + 1)
            if phase == 1:
                g.go(g.sibling(part, 0, g.me(part, 2)))
    for part in range(3):
        m = g.me(part, 2)
        g.sibling(part, 0, m, receive=True).wait_recv()
        for kind in range(2):
            g.sibling(part, 3 + kind, (m + 2) % 4, half=kind, receive=True).wait_recv()
        project(part, 0, pos, tok, w, acc3)
        p[part] = acc3[part].T.astype(BF).reshape(32, 16, 256)
    projs.start()
    for part in range(3):
        x[part, t] = p[part, t]
    my_cot.wait()
    cots.wait_recv()
    projs.wait_recv()

    conv_front(x, u, tap, wide, mpad, gpad)
    long_conv(mpad, s, acc)
    gate_and_query_grad(acc, u, wide, gated, grad)
    gates.start()
    my_gate = pltpu.make_async_copy(gated.at[t], gated_out.at[t], local.at[2])
    my_gate.start()
    query_back(tap, grad, pg)
    firsts.start()
    r[0, t] = pg[0, t]
    long_back(gpad, s, acc)
    key_value_back(acc, wide, tap, grad, pg)
    others.start()
    for part in (1, 2):
        r[part, t] = pg[part, t]

    filter_back(mpad, gpad, mt, z8, fmine)
    shares = []
    for d in range(1, 4):
        c = pltpu.make_async_remote_copy(
            src_ref=fmine,
            dst_ref=fgot.at[d],
            send_sem=f_send.at[d],
            recv_sem=f_recv.at[d],
            device_id=((f + d) % 4, t),
            device_id_type=MESH,
        )
        c.start()
        shares.append(c)

    firsts.wait_recv()
    pgt[0] = r[0].reshape(512, 256).astype(F32).T.astype(BF)

    @pl.loop(0, 16)
    def _(n):
        rhs = w[0, n // 8, n // 4 % 2, n % 4].reshape(512, 512)
        total[n] = lax.dot_general(pgt[0], rhs, DN_NT, preferred_element_type=F32)

    for c in shares:
        c.wait_recv()
    scale = 1.0 / math.sqrt(4 * 16 * 8192)
    filter_out[...] = ((fmine[...] + fgot[1]) + (fgot[2] + fgot[3])) * scale

    others.wait_recv()
    for part in (1, 2):
        pgt[part] = r[part].reshape(512, 256).astype(F32).T.astype(BF)

    def store(n):
        at = pl.ds(pl.multiple_of(512 * n, 512), 512)
        return pltpu.make_async_copy(tok.at[:, at], grad_out.at[:, at], out_sem.at[n])

    @pl.loop(0, 16)
    def _(n):
        one = w[1, n // 8, n // 4 % 2, n % 4].reshape(512, 512)
        two = w[2, n // 8, n // 4 % 2, n % 4].reshape(512, 512)
        out = lax.dot_general(
            jnp.concatenate([pgt[1], pgt[2]], axis=1),
            jnp.concatenate([one, two], axis=1),
            DN_NT,
            preferred_element_type=F32,
        )
        tok[:, pl.ds(pl.multiple_of(512 * n, 512), 512)] = (total[n] + out).astype(BF)
        store(n).start()

    my_gate.wait()
    gates.wait_recv()
    for e in (cots, projs, gates, firsts, others):
        e.wait_send()
    for c in shares:
        c.wait_send()
    g.wait_sends()

    @pl.loop(0, 16)
    def _(n):
        store(n).wait()


def body(tokens, projection, short_taps, long_filters, cotangent):
    vmem = pl.BlockSpec(memory_space=pltpu.VMEM)
    hbm = pl.BlockSpec(memory_space=pl.ANY)
    dma = pltpu.SemaphoreType.DMA
    gated, token_grad, filter_grad = pl.pallas_call(
        kernel,
        out_shape=[
            jax.ShapeDtypeStruct((32, 16, 256), BF),
            jax.ShapeDtypeStruct((256, 8192), BF),
            jax.ShapeDtypeStruct((1, 8192), F32),
        ],
        in_specs=[hbm, vmem, vmem, vmem, hbm],
        out_specs=[hbm, hbm, vmem],
        scratch_shapes=[
            pltpu.VMEM((3, 2, 2, 4, 4, 2, 64, 512), BF),
            pltpu.VMEM((256, 8192), BF),
            pltpu.VMEM((3, 256, 512), F32),
            pltpu.VMEM((3, 32, 16, 256), BF),
            pltpu.VMEM((3, 32, 16, 256), BF),
            pltpu.VMEM((32, 16, 256), BF),
            pltpu.VMEM((32, 256, 256), BF),
            pltpu.VMEM((9, 16, 256), F32),
            pltpu.VMEM((3, 32, 16, 256), F32),
            pltpu.VMEM((1024, 256), BF),
            pltpu.VMEM((1024, 256), BF),
            pltpu.VMEM((512, 256), F32),
            pltpu.VMEM((3, 33, 16, 256), F32),
            pltpu.VMEM((3, 32, 16, 256), BF),
            pltpu.VMEM((3, 32, 16, 256), BF),
            pltpu.VMEM((3, 256, 512), BF),
            pltpu.VMEM((256, 512), BF),
            pltpu.VMEM((8, 8448), F32),
            pltpu.VMEM((16, 256, 512), F32),
            pltpu.VMEM((32, 16, 256), BF),
            pltpu.VMEM((1, 8192), F32),
            pltpu.VMEM((4, 1, 8192), F32),
            dma((3,)),
            dma((3, 3, 4)),
            dma((3, 3, 4)),
            dma((3, 5)),
            dma((3, 5)),
            dma((3,)),
            dma((5, 32)),
            dma((5, 32)),
            dma((4,)),
            dma((4,)),
            dma((16,)),
        ],
        compiler_params=pltpu.CompilerParams(
            collective_id=0, has_side_effects=True, vmem_limit_bytes=62 * 1024 * 1024
        ),
    )(tokens[0], projection, short_taps, long_filters, cotangent[0].reshape(32, 16, 256))
    return gated.reshape(1, 512, 256), token_grad[None], filter_grad


def solution(mesh):
    in_specs = (
        P("fsdp", "ctx", None),
        P(("fsdp", "ctx"), None),
        P(),
        P("ctx", None),
        P("fsdp", None, "ctx"),
    )
    out_specs = (P("fsdp", None, "ctx"), P("fsdp", "ctx", None), P("ctx", None))
    return jax.shard_map(body, mesh=mesh, in_specs=in_specs, out_specs=out_specs, check_vma=False)
```

```python
import math

import jax
import jax.numpy as jnp
from jax import lax
from jax.experimental import pallas as pl
from jax.experimental.pallas import tpu as pltpu
from jax.sharding import PartitionSpec as P

MESH = pl.DeviceIdType.MESH
BF = jnp.bfloat16
F32 = jnp.float32
FULL = slice(None)
SUBS = (0, 3, 1, 2)
ORDERS = ((0, 1, 2), (1, 2, 0), (2, 0, 1))


def my_coords():
    f = lax.axis_index("fsdp")
    t = lax.axis_index("ctx")
    return f % 2, (t // 8, (t // 2) % 4, (t % 2) * 2 + f // 2)


def device_of(core, pos):
    z, x, y = pos
    return ((y % 2) * 2 + core, z * 8 + x * 2 + y // 2)


def moved(pos, axis, by):
    out = list(pos)
    out[axis] = (pos[axis] + by) % 4
    return tuple(out)


def shards(ref, part, core, pos, half=None):
    z, x, y = pos
    rows = FULL if half is None else pl.ds(half * 32, 32)
    yl = FULL if y is None else y % 2
    yh = FULL if y is None else y // 2
    z = FULL if z is None else z
    x = FULL if x is None else x
    return ref.at[part, yl, core, z, x, yh, rows, :]


class Gather:
    def __init__(self, w, own, send, recv, sib_send, sib_recv):
        self.w, self.own = w, own
        self.send, self.recv = send, recv
        self.sib_send, self.sib_recv = sib_send, sib_recv
        self.core, self.pos = my_coords()
        self.started = []

    def block(self, part, phase, at, half=None, core=None, sub=None):
        order = ORDERS[part]
        pos = [None, None, None]
        for later in order[phase + 1 :]:
            pos[later] = self.pos[later]
        pos[order[phase]] = at
        if sub is not None:
            pos[order[1]] = (self.pos[order[1]] + sub) % 4
        return shards(self.w, part, self.core if core is None else core, pos, half)

    def copy(self, part, phase, kind, at, by, half=None, sub=None):
        axis = ORDERS[part][phase]
        ref = self.block(part, phase, at, half, sub=sub)
        at = (part, phase, kind) if sub is None else (part, 2 + sub, kind)
        return pltpu.make_async_remote_copy(
            src_ref=ref,
            dst_ref=ref,
            send_sem=self.send.at[at],
            recv_sem=self.recv.at[at],
            device_id=device_of(self.core, moved(self.pos, axis, by)),
            device_id_type=MESH,
        )

    def go(self, c):
        c.start()
        self.started.append(c)

    def me(self, part, phase):
        return self.pos[ORDERS[part][phase]]

    def first(self, part, phase, sub=None):
        m = self.me(part, phase)
        self.go(self.copy(part, phase, 0, m, 1, sub=sub))
        self.go(self.copy(part, phase, 1, m, -1, sub=sub))

    def forward(self, part, phase, kind, sub=None):
        m = self.me(part, phase)
        by = 1 if kind == 0 else -1
        at = (m - by) % 4
        self.copy(part, phase, kind, at, by, sub=sub).wait_recv()
        self.go(self.copy(part, phase, 2 + kind, at, by, half=kind, sub=sub))
        if phase == 2:
            self.go(self.sibling(part, 1 + kind, sub))

    def last(self, part, phase, kind, sub=None):
        m = self.me(part, phase)
        self.copy(part, phase, 2 + kind, (m + 2) % 4, 1, half=kind, sub=sub).wait_recv()
        if phase == 2:
            self.go(self.sibling(part, 3 + kind, sub))

    def sibling(self, part, kind, sub, receive=False):
        core = 1 - self.core if receive else self.core
        at = (self.me(part, 2) + (0, -1, 1, 2, 2)[kind]) % 4
        ref = self.block(part, 2, at, None if kind < 3 else kind - 3, core, sub)
        return pltpu.make_async_remote_copy(
            src_ref=ref,
            dst_ref=ref,
            send_sem=self.sib_send.at[part, sub, kind],
            recv_sem=self.sib_recv.at[part, sub, kind],
            device_id=device_of(1 - self.core, self.pos),
            device_id_type=MESH,
        )

    def from_sibling(self, part, kinds):
        for sub in range(4):
            for kind in kinds:
                self.sibling(part, kind, sub, receive=True).wait_recv()

    def wait_sends(self):
        for c in self.started:
            c.wait_send()


DN_NT = (((1,), (1,)), ((), ()))
KK = 8


def lanes(shape):
    return lax.broadcasted_iota(jnp.int32, shape, len(shape) - 1)


def fill_toeplitz(h_ref, s_ref):
    @pl.loop(0, 32, unroll=2)
    def _(k):
        now = h_ref[:, pl.ds(pl.multiple_of(256 * k, 256), 256)]
        earlier = jnp.maximum(k - 1, 0)
        before = h_ref[:, pl.ds(pl.multiple_of(256 * earlier, 256), 256)]
        before = jnp.where(k > 0, before, 0.0)
        row = jnp.concatenate([before, now], axis=1)
        base = pltpu.roll(jnp.broadcast_to(row, (8, 512)), 0, 1, stride=1, stride_axis=0)
        for b in range(8):
            one = base if b == 0 else pltpu.roll(base, 16 * b, 1)
            two = pltpu.roll(base, 16 * b + 8, 1)
            pair = jnp.concatenate([one, two], axis=0).astype(BF)
            s_ref[k, 16 * b : 16 * b + 16, :] = pair[:, 256:512]
            s_ref[k, 128 + 16 * b : 144 + 16 * b, :] = pair[:, 128:384]


def fill_taps(taps_ref, tap_ref, group):
    lane = lanes((16, 512))
    chan = lax.broadcasted_iota(jnp.int32, (16, 512), 0)
    pick = (lane == group * 16 + chan).astype(F32)
    for tap in range(3):
        for part in range(3):
            row = taps_ref[tap : tap + 1, 512 * part : 512 * part + 512]
            col = jnp.sum(pick * row, axis=1, keepdims=True)
            tap_ref[3 * tap + part] = jnp.broadcast_to(col, (16, 256))


def conv_front(x_ref, u_ref, tap_ref, wide_ref, mpad_ref, gpad_ref):
    lane = lanes((16, 256))
    mpad_ref[0:512, :] = jnp.zeros((512, 256), BF)
    gpad_ref[512:1024, :] = jnp.zeros((512, 256), BF)

    @pl.loop(0, 32, unroll=4)
    def _(a):
        prev = jnp.maximum(a - 1, 0)
        got = []
        for part in range(3):
            x = x_ref[part, a].astype(F32)
            y = x_ref[part, prev].astype(F32)
            y = jnp.where(a > 0, y, 0.0)
            one = jnp.where(lane < 1, pltpu.roll(y, 1, 1), pltpu.roll(x, 1, 1))
            two = jnp.where(lane < 2, pltpu.roll(y, 2, 1), pltpu.roll(x, 2, 1))
            short = tap_ref[part] * x + tap_ref[3 + part] * one + tap_ref[6 + part] * two
            wide_ref[part, a] = short
            got.append(short)
        rows = pl.ds(pl.multiple_of(16 * a, 16), 16)
        later = pl.ds(pl.multiple_of(512 + 16 * a, 16), 16)
        mpad_ref[later, :] = (got[1] * got[2]).astype(BF)
        gpad_ref[rows, :] = (u_ref[a].astype(F32) * got[0]).astype(BF)


def long_conv(mpad_ref, s_ref, acc_ref):
    for n in range(32 // KK):
        low = 16 * KK * n
        lhs = [mpad_ref[512 + low - 16 * k : 1024 - 16 * k, :] for k in range(n * KK, n * KK + KK)]
        rhs = s_ref[n * KK : n * KK + KK].reshape(256 * KK, 256)
        out = jnp.dot(jnp.concatenate(lhs, axis=1), rhs, preferred_element_type=F32)
        if n == 0:
            acc_ref[...] = out
        else:
            acc_ref[low:512, :] += out


def long_back(gpad_ref, s_ref, acc_ref):
    for n in range(32 // KK):
        high = 512 - 16 * KK * n
        lhs = [gpad_ref[16 * k : 16 * k + high, :] for k in range(n * KK, n * KK + KK)]
        rhs = [s_ref[k] for k in range(n * KK, n * KK + KK)]
        out = lax.dot_general(
            jnp.concatenate(lhs, axis=1), jnp.concatenate(rhs, axis=1), DN_NT, preferred_element_type=F32
        )
        if n == 0:
            acc_ref[...] = out
        else:
            acc_ref[0:high, :] += out


def gate_and_query_grad(acc_ref, u_ref, wide_ref, gated_ref, grad_ref):
    @pl.loop(0, 32, unroll=4)
    def _(a):
        rows = pl.ds(pl.multiple_of(16 * a, 16), 16)
        conv = acc_ref[rows, :].astype(BF).astype(F32)
        gated_ref[a] = (wide_ref[0, a] * conv).astype(BF)
        grad_ref[0, a] = u_ref[a].astype(F32) * conv


def back_taps(part, a, tap_ref, grad_ref, pg_ref):
    lane = lanes((16, 256))
    x = grad_ref[part, a]
    y = grad_ref[part, a + 1]
    one = jnp.where(lane > 254, pltpu.roll(y, 255, 1), pltpu.roll(x, 255, 1))
    two = jnp.where(lane > 253, pltpu.roll(y, 254, 1), pltpu.roll(x, 254, 1))
    out = tap_ref[part] * x + tap_ref[3 + part] * one + tap_ref[6 + part] * two
    pg_ref[part, a] = out.astype(BF)


def query_back(tap_ref, grad_ref, pg_ref):
    grad_ref[:, 32] = jnp.zeros((3, 16, 256), F32)

    @pl.loop(0, 32, unroll=4)
    def _(a):
        back_taps(0, a, tap_ref, grad_ref, pg_ref)


def key_value_back(acc_ref, wide_ref, tap_ref, grad_ref, pg_ref):
    @pl.loop(0, 32, unroll=4)
    def _(a):
        rows = pl.ds(pl.multiple_of(16 * a, 16), 16)
        mg = acc_ref[rows, :].astype(BF).astype(F32)
        grad_ref[1, a] = mg * wide_ref[2, a]
        grad_ref[2, a] = mg * wide_ref[1, a]

    @pl.loop(0, 32, unroll=4)
    def _(a):
        back_taps(1, a, tap_ref, grad_ref, pg_ref)
        back_taps(2, a, tap_ref, grad_ref, pg_ref)


def filter_back(mpad_ref, gpad_ref, mt_ref, z_ref, out_ref):
    mt_ref[...] = mpad_ref[512:1024, :].astype(F32).T.astype(BF)
    for n in range(32 // KK):
        deep = 512 - 16 * KK * n

        @pl.loop(n * KK // 4, n * KK // 4 + KK // 4)
        def _(m):
            four = [gpad_ref[pl.ds(pl.multiple_of(64 * m + 16 * i, 16), deep), :] for i in range(4)]
            wide = jnp.dot(mt_ref[:, 0:deep], jnp.concatenate(four, axis=1), preferred_element_type=F32)
            for i in range(4):
                q = wide[:, 256 * i : 256 * i + 256]
                top, low = q[0:128], q[128:256]
                mid = top[:, 0:128] + low[:, 128:256]
                blank = jnp.zeros((128, 128), F32)
                x = jnp.concatenate([blank, low[:, 0:128], mid, top[:, 128:256]], axis=1)
                for half in (64, 32, 16, 8):
                    x = x[0:half] + pltpu.roll(x[half : 2 * half], 512 - half, 1)
                z_ref[4 * m + i] = x

    for k in range(32):
        x = z_ref[k, :, 256:512]
        y = z_ref[k + 1, :, 0:256] if k < 31 else jnp.zeros((8, 256), F32)
        after = z_ref[k + 1, :, 256:512] if k < 31 else jnp.zeros((8, 256), F32)
        if k < 30:
            after += z_ref[k + 2, :, 0:256]
        x = jnp.concatenate([x + y, after], axis=1)
        row = lax.broadcasted_iota(jnp.int32, x.shape, 0)
        for bit in (1, 2, 4):
            x = jnp.where(row // bit % 2 == 1, pltpu.roll(x, 512 - bit, 1), x)
        out_ref[:, 256 * k : 256 * k + 256] = jnp.sum(x[:, 0:256], axis=0, keepdims=True)


def each_peer(step):
    @pl.loop(1, 32)
    def _(d):
        step(d)


class Exchange:
    def __init__(self, src, dst, send, recv):
        self.src, self.dst, self.send, self.recv = src, dst, send, recv
        self.f, self.t = lax.axis_index("fsdp"), lax.axis_index("ctx")

    def copy(self, d):
        peer = (self.t + d) % 32
        return pltpu.make_async_remote_copy(
            src_ref=self.src(peer),
            dst_ref=self.dst(self.t),
            send_sem=self.send.at[d],
            recv_sem=self.recv.at[d],
            device_id=(self.f, peer),
            device_id_type=MESH,
        )

    def start(self):
        each_peer(lambda d: self.copy(d).start())

    def wait_recv(self):
        each_peer(lambda d: self.copy(d).wait_recv())

    def wait_send(self):
        each_peer(lambda d: self.copy(d).wait_send())


def project(part, near, pos, tok, w, acc):
    z, x, y = pos
    for n in range(2):
        left, right = [], []

        def piece(row, size, block):
            left.append(tok[:, pl.ds(pl.multiple_of(row * size, size), size)])
            right.append(block.reshape(size, 512))

        if part == 0:
            fy = (y + near) % 2
            piece(fy * 2 + n, 2048, w[part, fy, n])
        else:
            for fc in range(2):
                for hop in (0, 2):
                    if part == 1:
                        fz = (z + near + hop) % 4
                        piece((n * 2 + fc) * 4 + fz, 512, w[part, n, fc, fz])
                    else:
                        fx = (x + near + hop) % 4
                        for fz in range(4):
                            piece(((n * 2 + fc) * 4 + fz) * 4 + fx, 128, w[part, n, fc, fz, fx])
        lhs = jnp.concatenate(left, axis=1)
        acc[part] += jnp.dot(lhs, jnp.concatenate(right, axis=0), preferred_element_type=F32)


def kernel(
    tok_hbm, own, taps, h, cot_hbm,
    gated_out, grad_out, filter_out,
    w, tok, acc3, p, x, u, s, tap, wide, mpad, gpad, acc, grad, pg, r, mt, z8, total, gated, fmine, fgot,
    put, send, recv, sib_send, sib_recv, local, a2a_send, a2a_recv, f_send, f_recv, out_sem,
):
    g = Gather(w, own, send, recv, sib_send, sib_recv)
    f, t = lax.axis_index("fsdp"), lax.axis_index("ctx")
    core, pos = g.core, g.pos
    barrier = pltpu.get_barrier_semaphore()

    def hello(device):
        pl.semaphore_signal(barrier, inc=1, device_id=device, device_id_type=MESH)

    each_peer(lambda d: hello((f, (t + d) % 32)))
    for d in range(1, 4):
        hello(((f + d) % 4, t))
    hello(((f + 2) % 4, t + 1 - t % 2 * 2))
    load = pltpu.make_async_copy(tok_hbm, tok, local.at[0])
    load.start()
    mine = []
    for part in range(3):
        c = pltpu.make_async_copy(
            own.at[:, pl.ds(512 * part, 512)], shards(w, part, core, pos), put.at[part]
        )
        c.start()
        mine.append(c)
    my_cot = pltpu.make_async_copy(cot_hbm.at[t], u.at[t], local.at[1])
    my_cot.start()
    for c in mine:
        c.wait()
    pl.semaphore_wait(barrier, 35)

    cots = Exchange(lambda q: cot_hbm.at[q], lambda q: u.at[q], a2a_send.at[0], a2a_recv.at[0])
    projs = Exchange(lambda q: p.at[:, q], lambda q: x.at[:, q], a2a_send.at[1], a2a_recv.at[1])
    gates = Exchange(lambda q: gated.at[q], lambda q: gated_out.at[q], a2a_send.at[2], a2a_recv.at[2])
    firsts = Exchange(lambda q: pg.at[0, q], lambda q: r.at[0, q], a2a_send.at[3], a2a_recv.at[3])
    others = Exchange(
        lambda q: pg.at[pl.ds(1, 2), q], lambda q: r.at[pl.ds(1, 2), q], a2a_send.at[4], a2a_recv.at[4]
    )

    parts = range(3)
    for part in parts:
        g.first(part, 0)
    fill_taps(taps, tap, t)
    acc3[...] = jnp.zeros_like(acc3)
    for kind in range(2):
        for part in parts:
            g.forward(part, 0, kind)
    for part in parts:
        for kind in range(2):
            g.last(part, 0, kind)
        g.first(part, 1)
        g.first(part, 2, 0)
        g.go(g.sibling(part, 0, 0))
    for kind in range(2):
        for part in parts:
            g.forward(part, 1, kind)
            g.first(part, 2, SUBS[1 + kind])
            g.go(g.sibling(part, 0, SUBS[1 + kind]))
    for part in parts:
        for kind in range(2):
            g.last(part, 1, kind)
        g.first(part, 2, 2)
        g.go(g.sibling(part, 0, 2))
    fill_toeplitz(h, s)
    for kind in range(2):
        for part in parts:
            g.forward(part, 2, kind, 0)
    cots.start()
    load.wait()
    for sub in SUBS[1:]:
        for kind in range(2):
            for part in parts:
                g.forward(part, 2, kind, sub)
    for sub in SUBS[:2]:
        for part in parts:
            for kind in range(2):
                g.last(part, 2, kind, sub)
    for part in parts:
        g.from_sibling(part, (1, 2))
        project(part, 1, pos, tok, w, acc3)
    for sub in SUBS[2:]:
        for part in parts:
            for kind in range(2):
                g.last(part, 2, kind, sub)
    for part in parts:
        g.from_sibling(part, (0, 3, 4))
        project(part, 0, pos, tok, w, acc3)
        p[part] = acc3[part].T.astype(BF).reshape(32, 16, 256)
    projs.start()
    for part in range(3):
        x[part, t] = p[part, t]
    my_cot.wait()
    cots.wait_recv()
    projs.wait_recv()

    conv_front(x, u, tap, wide, mpad, gpad)
    long_conv(mpad, s, acc)
    gate_and_query_grad(acc, u, wide, gated, grad)
    gates.start()
    my_gate = pltpu.make_async_copy(gated.at[t], gated_out.at[t], local.at[2])
    my_gate.start()
    query_back(tap, grad, pg)
    firsts.start()
    r[0, t] = pg[0, t]
    long_back(gpad, s, acc)
    key_value_back(acc, wide, tap, grad, pg)
    others.start()
    for part in (1, 2):
        r[part, t] = pg[part, t]

    filter_back(mpad, gpad, mt, z8, fmine)
    shares = []
    for d in range(1, 4):
        c = pltpu.make_async_remote_copy(
            src_ref=fmine,
            dst_ref=fgot.at[d],
            send_sem=f_send.at[d],
            recv_sem=f_recv.at[d],
            device_id=((f + d) % 4, t),
            device_id_type=MESH,
        )
        c.start()
        shares.append(c)

    def weights(part, n):
        return w[part, n // 4, n // 2 % 2, pl.ds(n % 2 * 2, 2)].reshape(1024, 512)

    firsts.wait_recv()

    @pl.loop(0, 8)
    def _(n):
        total[n] = jnp.dot(weights(0, n), r[0].reshape(512, 256), preferred_element_type=F32)

    for c in shares:
        c.wait_recv()
    scale = 1.0 / math.sqrt(4 * 16 * 8192)
    filter_out[...] = ((fmine[...] + fgot[1]) + (fgot[2] + fgot[3])) * scale

    others.wait_recv()

    def store(n):
        at = pl.ds(pl.multiple_of(1024 * n, 1024), 1024)
        return pltpu.make_async_copy(tok.at[:, at], grad_out.at[:, at], out_sem.at[n])

    @pl.loop(0, 8)
    def _(n):
        lhs = jnp.concatenate([weights(1, n), weights(2, n)], axis=1)
        out = total[n] + jnp.dot(lhs, r[1:3].reshape(1024, 256), preferred_element_type=F32)
        tok[:, pl.ds(pl.multiple_of(1024 * n, 1024), 1024)] = out.astype(BF).T
        store(n).start()

    my_gate.wait()
    gates.wait_recv()
    for e in (cots, projs, gates, firsts, others):
        e.wait_send()
    for c in shares:
        c.wait_send()
    g.wait_sends()

    @pl.loop(0, 8)
    def _(n):
        store(n).wait()


def body(tokens, projection, short_taps, long_filters, cotangent):
    vmem = pl.BlockSpec(memory_space=pltpu.VMEM)
    hbm = pl.BlockSpec(memory_space=pl.ANY)
    dma = pltpu.SemaphoreType.DMA
    gated, token_grad, filter_grad = pl.pallas_call(
        kernel,
        out_shape=[
            jax.ShapeDtypeStruct((32, 16, 256), BF),
            jax.ShapeDtypeStruct((256, 8192), BF),
            jax.ShapeDtypeStruct((1, 8192), F32),
        ],
        in_specs=[hbm, vmem, vmem, vmem, hbm],
        out_specs=[hbm, hbm, vmem],
        scratch_shapes=[
            pltpu.VMEM((3, 2, 2, 4, 4, 2, 64, 512), BF),
            pltpu.VMEM((256, 8192), BF),
            pltpu.VMEM((3, 256, 512), F32),
            pltpu.VMEM((3, 32, 16, 256), BF),
            pltpu.VMEM((3, 32, 16, 256), BF),
            pltpu.VMEM((32, 16, 256), BF),
            pltpu.VMEM((32, 256, 256), BF),
            pltpu.VMEM((9, 16, 256), F32),
            pltpu.VMEM((3, 32, 16, 256), F32),
            pltpu.VMEM((1024, 256), BF),
            pltpu.VMEM((1024, 256), BF),
            pltpu.VMEM((512, 256), F32),
            pltpu.VMEM((3, 33, 16, 256), F32),
            pltpu.VMEM((3, 32, 16, 256), BF),
            pltpu.VMEM((3, 32, 16, 256), BF),
            pltpu.VMEM((256, 512), BF),
            pltpu.VMEM((32, 8, 512), F32),
            pltpu.VMEM((8, 1024, 256), F32),
            pltpu.VMEM((32, 16, 256), BF),
            pltpu.VMEM((1, 8192), F32),
            pltpu.VMEM((4, 1, 8192), F32),
            dma((3,)),
            dma((3, 6, 4)),
            dma((3, 6, 4)),
            dma((3, 4, 5)),
            dma((3, 4, 5)),
            dma((3,)),
            dma((5, 32)),
            dma((5, 32)),
            dma((4,)),
            dma((4,)),
            dma((8,)),
        ],
        compiler_params=pltpu.CompilerParams(
            collective_id=0, has_side_effects=True, vmem_limit_bytes=62 * 1024 * 1024
        ),
    )(tokens[0], projection, short_taps, long_filters, cotangent[0].reshape(32, 16, 256))
    return gated.reshape(1, 512, 256), token_grad[None], filter_grad


def solution(mesh):
    in_specs = (
        P("fsdp", "ctx", None),
        P(("fsdp", "ctx"), None),
        P(),
        P("ctx", None),
        P("fsdp", None, "ctx"),
    )
    out_specs = (P("fsdp", None, "ctx"), P("fsdp", "ctx", None), P("ctx", None))
    return jax.shard_map(body, mesh=mesh, in_specs=in_specs, out_specs=out_specs, check_vma=False)
```

```python
import math

import jax
import jax.numpy as jnp
from jax import lax
from jax.experimental import pallas as pl
from jax.experimental.pallas import tpu as pltpu
from jax.sharding import PartitionSpec as P

MESH = pl.DeviceIdType.MESH
BF = jnp.bfloat16
F32 = jnp.float32
FULL = slice(None)
SUBS = (0, 3, 1, 2)
ORDERS = ((0, 1, 2), (1, 2, 0), (2, 0, 1))


def my_coords():
    f = lax.axis_index("fsdp")
    t = lax.axis_index("ctx")
    return f % 2, (t // 8, (t // 2) % 4, (t % 2) * 2 + f // 2)


def device_of(core, pos):
    z, x, y = pos
    return ((y % 2) * 2 + core, z * 8 + x * 2 + y // 2)


def moved(pos, axis, by):
    out = list(pos)
    out[axis] = (pos[axis] + by) % 4
    return tuple(out)


def shards(ref, part, core, pos, half=None):
    z, x, y = pos
    rows = FULL if half is None else pl.ds(half * 32, 32)
    yl = FULL if y is None else y % 2
    yh = FULL if y is None else y // 2
    z = FULL if z is None else z
    x = FULL if x is None else x
    return ref.at[part, yl, core, z, x, yh, rows, :]


class Gather:
    def __init__(self, w, own, send, recv, sib_send, sib_recv):
        self.w, self.own = w, own
        self.send, self.recv = send, recv
        self.sib_send, self.sib_recv = sib_send, sib_recv
        self.core, self.pos = my_coords()
        self.started = []

    def block(self, part, phase, at, half=None, core=None, sub=None):
        order = ORDERS[part]
        pos = [None, None, None]
        for later in order[phase + 1 :]:
            pos[later] = self.pos[later]
        pos[order[phase]] = at
        if sub is not None:
            pos[order[1]] = (self.pos[order[1]] + sub) % 4
        return shards(self.w, part, self.core if core is None else core, pos, half)

    def copy(self, part, phase, kind, at, by, half=None, sub=None):
        axis = ORDERS[part][phase]
        ref = self.block(part, phase, at, half, sub=sub)
        at = (part, phase, kind) if sub is None else (part, 2 + sub, kind)
        return pltpu.make_async_remote_copy(
            src_ref=ref,
            dst_ref=ref,
            send_sem=self.send.at[at],
            recv_sem=self.recv.at[at],
            device_id=device_of(self.core, moved(self.pos, axis, by)),
            device_id_type=MESH,
        )

    def go(self, c):
        c.start()
        self.started.append(c)

    def me(self, part, phase):
        return self.pos[ORDERS[part][phase]]

    def first(self, part, phase, sub=None):
        m = self.me(part, phase)
        self.go(self.copy(part, phase, 0, m, 1, sub=sub))
        self.go(self.copy(part, phase, 1, m, -1, sub=sub))

    def forward(self, part, phase, kind, sub=None):
        m = self.me(part, phase)
        by = 1 if kind == 0 else -1
        at = (m - by) % 4
        self.copy(part, phase, kind, at, by, sub=sub).wait_recv()
        self.go(self.copy(part, phase, 2 + kind, at, by, half=kind, sub=sub))
        if phase == 2:
            self.go(self.sibling(part, 1 + kind, sub))

    def last(self, part, phase, kind, sub=None):
        m = self.me(part, phase)
        self.copy(part, phase, 2 + kind, (m + 2) % 4, 1, half=kind, sub=sub).wait_recv()
        if phase == 2:
            self.go(self.sibling(part, 3 + kind, sub))

    def sibling(self, part, kind, sub, receive=False):
        core = 1 - self.core if receive else self.core
        at = (self.me(part, 2) + (0, -1, 1, 2, 2)[kind]) % 4
        ref = self.block(part, 2, at, None if kind < 3 else kind - 3, core, sub)
        return pltpu.make_async_remote_copy(
            src_ref=ref,
            dst_ref=ref,
            send_sem=self.sib_send.at[part, sub, kind],
            recv_sem=self.sib_recv.at[part, sub, kind],
            device_id=device_of(1 - self.core, self.pos),
            device_id_type=MESH,
        )

    def from_sibling(self, part, kinds, subs):
        for sub in subs:
            for kind in kinds:
                self.sibling(part, kind, sub, receive=True).wait_recv()

    def wait_sends(self):
        for c in self.started:
            c.wait_send()


DN_NT = (((1,), (1,)), ((), ()))
KK = 8


def lanes(shape):
    return lax.broadcasted_iota(jnp.int32, shape, len(shape) - 1)


def fill_toeplitz(h_ref, s_ref):
    @pl.loop(0, 32, unroll=2)
    def _(k):
        now = h_ref[:, pl.ds(pl.multiple_of(256 * k, 256), 256)]
        earlier = jnp.maximum(k - 1, 0)
        before = h_ref[:, pl.ds(pl.multiple_of(256 * earlier, 256), 256)]
        before = jnp.where(k > 0, before, 0.0)
        row = jnp.concatenate([before, now], axis=1)
        base = pltpu.roll(jnp.broadcast_to(row, (8, 512)), 0, 1, stride=1, stride_axis=0)
        for b in range(8):
            one = base if b == 0 else pltpu.roll(base, 16 * b, 1)
            two = pltpu.roll(base, 16 * b + 8, 1)
            pair = jnp.concatenate([one, two], axis=0).astype(BF)
            s_ref[k, 16 * b : 16 * b + 16, :] = pair[:, 256:512]
            s_ref[k, 128 + 16 * b : 144 + 16 * b, :] = pair[:, 128:384]


def fill_taps(taps_ref, tap_ref, group):
    lane = lanes((16, 512))
    chan = lax.broadcasted_iota(jnp.int32, (16, 512), 0)
    pick = (lane == group * 16 + chan).astype(F32)
    for tap in range(3):
        for part in range(3):
            row = taps_ref[tap : tap + 1, 512 * part : 512 * part + 512]
            col = jnp.sum(pick * row, axis=1, keepdims=True)
            tap_ref[3 * tap + part] = jnp.broadcast_to(col, (16, 256))


def conv_front(x_ref, u_ref, tap_ref, wide_ref, mpad_ref, gpad_ref):
    lane = lanes((16, 256))
    mpad_ref[0:512, :] = jnp.zeros((512, 256), BF)
    gpad_ref[512:1024, :] = jnp.zeros((512, 256), BF)

    @pl.loop(0, 32, unroll=4)
    def _(a):
        prev = jnp.maximum(a - 1, 0)
        got = []
        for part in range(3):
            x = x_ref[part, a].astype(F32)
            y = x_ref[part, prev].astype(F32)
            y = jnp.where(a > 0, y, 0.0)
            one = jnp.where(lane < 1, pltpu.roll(y, 1, 1), pltpu.roll(x, 1, 1))
            two = jnp.where(lane < 2, pltpu.roll(y, 2, 1), pltpu.roll(x, 2, 1))
            short = tap_ref[part] * x + tap_ref[3 + part] * one + tap_ref[6 + part] * two
            wide_ref[part, a] = short
            got.append(short)
        rows = pl.ds(pl.multiple_of(16 * a, 16), 16)
        later = pl.ds(pl.multiple_of(512 + 16 * a, 16), 16)
        mpad_ref[later, :] = (got[1] * got[2]).astype(BF)
        gpad_ref[rows, :] = (u_ref[a].astype(F32) * got[0]).astype(BF)


def long_conv(mpad_ref, s_ref, acc_ref):
    for n in range(32 // KK):
        low = 16 * KK * n
        lhs = [mpad_ref[512 + low - 16 * k : 1024 - 16 * k, :] for k in range(n * KK, n * KK + KK)]
        rhs = s_ref[n * KK : n * KK + KK].reshape(256 * KK, 256)
        out = jnp.dot(jnp.concatenate(lhs, axis=1), rhs, preferred_element_type=F32)
        if n == 0:
            acc_ref[...] = out
        else:
            acc_ref[low:512, :] += out


def long_back(gpad_ref, s_ref, acc_ref):
    for n in range(32 // KK):
        high = 512 - 16 * KK * n
        lhs = [gpad_ref[16 * k : 16 * k + high, :] for k in range(n * KK, n * KK + KK)]
        rhs = [s_ref[k] for k in range(n * KK, n * KK + KK)]
        out = lax.dot_general(
            jnp.concatenate(lhs, axis=1), jnp.concatenate(rhs, axis=1), DN_NT, preferred_element_type=F32
        )
        if n == 0:
            acc_ref[...] = out
        else:
            acc_ref[0:high, :] += out


def gate_and_query_grad(acc_ref, u_ref, wide_ref, gated_ref, grad_ref):
    @pl.loop(0, 32, unroll=4)
    def _(a):
        rows = pl.ds(pl.multiple_of(16 * a, 16), 16)
        conv = acc_ref[rows, :].astype(BF).astype(F32)
        gated_ref[a] = (wide_ref[0, a] * conv).astype(BF)
        grad_ref[0, a] = u_ref[a].astype(F32) * conv


def back_taps(part, a, tap_ref, grad_ref, pg_ref):
    lane = lanes((16, 256))
    x = grad_ref[part, a]
    y = grad_ref[part, a + 1]
    one = jnp.where(lane > 254, pltpu.roll(y, 255, 1), pltpu.roll(x, 255, 1))
    two = jnp.where(lane > 253, pltpu.roll(y, 254, 1), pltpu.roll(x, 254, 1))
    out = tap_ref[part] * x + tap_ref[3 + part] * one + tap_ref[6 + part] * two
    pg_ref[part, a] = out.astype(BF)


def query_back(tap_ref, grad_ref, pg_ref):
    @pl.loop(0, 32, unroll=4)
    def _(a):
        back_taps(0, a, tap_ref, grad_ref, pg_ref)


def key_value_back(acc_ref, wide_ref, tap_ref, grad_ref, pg_ref):
    grad_ref[:, 32] = jnp.zeros((3, 16, 256), F32)

    @pl.loop(0, 32, unroll=4)
    def _(a):
        rows = pl.ds(pl.multiple_of(16 * a, 16), 16)
        mg = acc_ref[rows, :].astype(BF).astype(F32)
        grad_ref[1, a] = mg * wide_ref[2, a]
        grad_ref[2, a] = mg * wide_ref[1, a]

    @pl.loop(0, 32, unroll=4)
    def _(a):
        back_taps(1, a, tap_ref, grad_ref, pg_ref)
        back_taps(2, a, tap_ref, grad_ref, pg_ref)


def filter_back(mpad_ref, gpad_ref, mt_ref, z_ref, out_ref):
    mt_ref[...] = mpad_ref[512:1024, :].astype(F32).T.astype(BF)
    for n in range(32 // KK):
        deep = 512 - 16 * KK * n

        @pl.loop(n * KK // 4, n * KK // 4 + KK // 4)
        def _(m):
            four = [gpad_ref[pl.ds(pl.multiple_of(64 * m + 16 * i, 16), deep), :] for i in range(4)]
            wide = jnp.dot(mt_ref[:, 0:deep], jnp.concatenate(four, axis=1), preferred_element_type=F32)
            for i in range(4):
                q = wide[:, 256 * i : 256 * i + 256]
                top, low = q[0:128], q[128:256]
                mid = top[:, 0:128] + low[:, 128:256]
                blank = jnp.zeros((128, 128), F32)
                x = jnp.concatenate([blank, low[:, 0:128], mid, top[:, 128:256]], axis=1)
                for half in (64, 32, 16, 8):
                    x = x[0:half] + pltpu.roll(x[half : 2 * half], 512 - half, 1)
                z_ref[4 * m + i] = x

    for k in range(32):
        x = z_ref[k, :, 256:512]
        y = z_ref[k + 1, :, 0:256] if k < 31 else jnp.zeros((8, 256), F32)
        after = z_ref[k + 1, :, 256:512] if k < 31 else jnp.zeros((8, 256), F32)
        if k < 30:
            after += z_ref[k + 2, :, 0:256]
        x = jnp.concatenate([x + y, after], axis=1)
        row = lax.broadcasted_iota(jnp.int32, x.shape, 0)
        for bit in (1, 2, 4):
            x = jnp.where(row // bit % 2 == 1, pltpu.roll(x, 512 - bit, 1), x)
        out_ref[:, 256 * k : 256 * k + 256] = jnp.sum(x[:, 0:256], axis=0, keepdims=True)


def each_peer(step, unroll=1):
    @pl.loop(1, 32, unroll=unroll)
    def _(d):
        step(d)


class Exchange:
    def __init__(self, src, dst, send, recv):
        self.src, self.dst, self.send, self.recv = src, dst, send, recv
        self.f, self.t = lax.axis_index("fsdp"), lax.axis_index("ctx")

    def copy(self, d):
        peer = (self.t + d) % 32
        return pltpu.make_async_remote_copy(
            src_ref=self.src(peer),
            dst_ref=self.dst(self.t),
            send_sem=self.send.at[d],
            recv_sem=self.recv.at[d],
            device_id=(self.f, peer),
            device_id_type=MESH,
        )

    def start(self):
        each_peer(lambda d: self.copy(d).start(), 31)

    def wait_recv(self):
        each_peer(lambda d: self.copy(d).wait_recv())

    def wait_send(self):
        each_peer(lambda d: self.copy(d).wait_send())


def project(part, near, subs, pos, tok, w, acc):
    z, x, y = pos
    left, right = [], []

    def piece(row, size, block):
        left.append(tok[:, pl.ds(pl.multiple_of(row * size, size), size)])
        right.append(block.reshape(size, 512))

    for fc in range(2):
        if part == 0:
            fy = (y + near) % 2
            if len(subs) == 4:
                piece(fy * 2 + fc, 2048, w[part, fy, fc])
            else:
                for sub in subs:
                    fx = (x + sub) % 4
                    for fz in range(4):
                        piece(((fy * 2 + fc) * 4 + fz) * 4 + fx, 128, w[part, fy, fc, fz, fx])
        for hop in (0, 2):
            if part == 1:
                fz = (z + near + hop) % 4
                for sub in subs:
                    if sub < 2:
                        fy = (y + sub) % 2
                        piece((fy * 2 + fc) * 4 + fz, 512, w[part, fy, fc, fz])
            if part == 2:
                fx = (x + near + hop) % 4
                for fy in range(2):
                    for sub in subs:
                        fz = (z + sub) % 4
                        piece(((fy * 2 + fc) * 4 + fz) * 4 + fx, 128, w[part, fy, fc, fz, fx])
    acc[part] += jnp.dot(
        jnp.concatenate(left, axis=1), jnp.concatenate(right, axis=0), preferred_element_type=F32
    )


def kernel(
    tok_hbm, own, taps, h, cot_hbm,
    gated_out, grad_out, filter_out,
    w, tok, acc3, p, x, u, s, tap, wide, mpad, gpad, acc, grad, pg, r, mt, z8, total, gated, fmine, fgot,
    put, send, recv, sib_send, sib_recv, local, a2a_send, a2a_recv, f_send, f_recv, out_sem,
):
    g = Gather(w, own, send, recv, sib_send, sib_recv)
    f, t = lax.axis_index("fsdp"), lax.axis_index("ctx")
    core, pos = g.core, g.pos
    barrier = pltpu.get_barrier_semaphore()

    def hello(device):
        pl.semaphore_signal(barrier, inc=1, device_id=device, device_id_type=MESH)

    for axis in range(3):
        for by in (1, -1):
            hello(device_of(core, moved(pos, axis, by)))
    hello(device_of(1 - core, pos))
    load = pltpu.make_async_copy(tok_hbm, tok, local.at[0])
    load.start()
    mine = []
    for part in range(3):
        c = pltpu.make_async_copy(
            own.at[:, pl.ds(512 * part, 512)], shards(w, part, core, pos), put.at[part]
        )
        c.start()
        mine.append(c)
    my_cot = pltpu.make_async_copy(cot_hbm.at[t], u.at[t], local.at[1])
    my_cot.start()
    for c in mine:
        c.wait()
    pl.semaphore_wait(barrier, 7)

    cots = Exchange(lambda q: cot_hbm.at[q], lambda q: u.at[q], a2a_send.at[0], a2a_recv.at[0])
    projs = Exchange(lambda q: p.at[:, q], lambda q: x.at[:, q], a2a_send.at[1], a2a_recv.at[1])
    gates = Exchange(lambda q: gated.at[q], lambda q: gated_out.at[q], a2a_send.at[2], a2a_recv.at[2])
    firsts = Exchange(lambda q: pg.at[0, q], lambda q: r.at[0, q], a2a_send.at[3], a2a_recv.at[3])
    others = Exchange(
        lambda q: pg.at[pl.ds(1, 2), q], lambda q: r.at[pl.ds(1, 2), q], a2a_send.at[4], a2a_recv.at[4]
    )

    parts = range(3)
    for part in parts:
        g.first(part, 0)
    fill_taps(taps, tap, t)
    acc3[...] = jnp.zeros_like(acc3)
    for kind in range(2):
        for part in parts:
            g.forward(part, 0, kind)
    for part in parts:
        for kind in range(2):
            g.last(part, 0, kind)
        g.first(part, 1)
        g.first(part, 2, 0)
        g.go(g.sibling(part, 0, 0))
    for kind in range(2):
        for part in parts:
            g.forward(part, 1, kind)
            g.first(part, 2, SUBS[1 + kind])
            g.go(g.sibling(part, 0, SUBS[1 + kind]))
    for part in parts:
        for kind in range(2):
            g.last(part, 1, kind)
        g.first(part, 2, 2)
        g.go(g.sibling(part, 0, 2))
    fill_toeplitz(h, s)
    for kind in range(2):
        for part in parts:
            g.forward(part, 2, kind, 0)
    load.wait()
    for sub in SUBS[1:]:
        for kind in range(2):
            for part in parts:
                g.forward(part, 2, kind, sub)
    def lasts(subs):
        for sub in subs:
            for part in parts:
                for kind in range(2):
                    g.last(part, 2, kind, sub)

    lasts(SUBS[:2])
    for part in parts:
        g.from_sibling(part, (1, 2), SUBS)
        project(part, 1, SUBS, pos, tok, w, acc3)
    lasts(SUBS[2:3])
    for part in (1, 0, 2):
        g.from_sibling(part, (0, 3, 4), SUBS[:3])
        project(part, 0, SUBS[1:3] if part == 1 else SUBS[:3], pos, tok, w, acc3)
    lasts(SUBS[3:])
    cots.start()
    for part in parts:
        g.from_sibling(part, (0, 3, 4), SUBS[3:])
        project(part, 0, (0, 2) if part == 1 else SUBS[3:], pos, tok, w, acc3)
        p[part] = acc3[part].T.astype(BF).reshape(32, 16, 256)
    projs.start()
    for part in range(3):
        x[part, t] = p[part, t]
    my_cot.wait()
    cots.wait_recv()
    projs.wait_recv()

    conv_front(x, u, tap, wide, mpad, gpad)
    long_back(gpad, s, acc)
    key_value_back(acc, wide, tap, grad, pg)
    others.start()
    for part in (1, 2):
        r[part, t] = pg[part, t]
    long_conv(mpad, s, acc)
    gate_and_query_grad(acc, u, wide, gated, grad)
    query_back(tap, grad, pg)
    firsts.start()
    r[0, t] = pg[0, t]
    gates.start()
    my_gate = pltpu.make_async_copy(gated.at[t], gated_out.at[t], local.at[2])
    my_gate.start()

    filter_back(mpad, gpad, mt, z8, fmine)
    shares = []
    for d in range(1, 4):
        c = pltpu.make_async_remote_copy(
            src_ref=fmine,
            dst_ref=fgot.at[d],
            send_sem=f_send.at[d],
            recv_sem=f_recv.at[d],
            device_id=((f + d) % 4, t),
            device_id_type=MESH,
        )
        c.start()
        shares.append(c)

    def weights(part, n):
        return w[part, n // 4, n // 2 % 2, pl.ds(n % 2 * 2, 2)].reshape(1024, 512)

    others.wait_recv()

    @pl.loop(0, 8)
    def _(n):
        lhs = jnp.concatenate([weights(1, n), weights(2, n)], axis=1)
        total[n] = jnp.dot(lhs, r[1:3].reshape(1024, 256), preferred_element_type=F32)

    for c in shares:
        c.wait_recv()
    scale = 1.0 / math.sqrt(4 * 16 * 8192)
    filter_out[...] = ((fmine[...] + fgot[1]) + (fgot[2] + fgot[3])) * scale

    firsts.wait_recv()

    def store(n):
        at = pl.ds(pl.multiple_of(1024 * n, 1024), 1024)
        return pltpu.make_async_copy(tok.at[:, at], grad_out.at[:, at], out_sem.at[n])

    @pl.loop(0, 8)
    def _(n):
        out = total[n] + jnp.dot(weights(0, n), r[0].reshape(512, 256), preferred_element_type=F32)
        tok[:, pl.ds(pl.multiple_of(1024 * n, 1024), 1024)] = out.astype(BF).T
        store(n).start()

    my_gate.wait()
    gates.wait_recv()
    for e in (cots, projs, gates, firsts, others):
        e.wait_send()
    for c in shares:
        c.wait_send()
    g.wait_sends()

    @pl.loop(0, 8)
    def _(n):
        store(n).wait()


def body(tokens, projection, short_taps, long_filters, cotangent):
    vmem = pl.BlockSpec(memory_space=pltpu.VMEM)
    hbm = pl.BlockSpec(memory_space=pl.ANY)
    dma = pltpu.SemaphoreType.DMA
    gated, token_grad, filter_grad = pl.pallas_call(
        kernel,
        out_shape=[
            jax.ShapeDtypeStruct((32, 16, 256), BF),
            jax.ShapeDtypeStruct((256, 8192), BF),
            jax.ShapeDtypeStruct((1, 8192), F32),
        ],
        in_specs=[hbm, vmem, vmem, vmem, hbm],
        out_specs=[hbm, hbm, vmem],
        scratch_shapes=[
            pltpu.VMEM((3, 2, 2, 4, 4, 2, 64, 512), BF),
            pltpu.VMEM((256, 8192), BF),
            pltpu.VMEM((3, 256, 512), F32),
            pltpu.VMEM((3, 32, 16, 256), BF),
            pltpu.VMEM((3, 32, 16, 256), BF),
            pltpu.VMEM((32, 16, 256), BF),
            pltpu.VMEM((32, 256, 256), BF),
            pltpu.VMEM((9, 16, 256), F32),
            pltpu.VMEM((3, 32, 16, 256), F32),
            pltpu.VMEM((1024, 256), BF),
            pltpu.VMEM((1024, 256), BF),
            pltpu.VMEM((512, 256), F32),
            pltpu.VMEM((3, 33, 16, 256), F32),
            pltpu.VMEM((3, 32, 16, 256), BF),
            pltpu.VMEM((3, 32, 16, 256), BF),
            pltpu.VMEM((256, 512), BF),
            pltpu.VMEM((32, 8, 512), F32),
            pltpu.VMEM((8, 1024, 256), F32),
            pltpu.VMEM((32, 16, 256), BF),
            pltpu.VMEM((1, 8192), F32),
            pltpu.VMEM((4, 1, 8192), F32),
            dma((3,)),
            dma((3, 6, 4)),
            dma((3, 6, 4)),
            dma((3, 4, 5)),
            dma((3, 4, 5)),
            dma((3,)),
            dma((5, 32)),
            dma((5, 32)),
            dma((4,)),
            dma((4,)),
            dma((8,)),
        ],
        compiler_params=pltpu.CompilerParams(
            collective_id=0, has_side_effects=True, vmem_limit_bytes=62 * 1024 * 1024
        ),
    )(tokens[0], projection, short_taps, long_filters, cotangent[0].reshape(32, 16, 256))
    return gated.reshape(1, 512, 256), token_grad[None], filter_grad


def solution(mesh):
    in_specs = (
        P("fsdp", "ctx", None),
        P(("fsdp", "ctx"), None),
        P(),
        P("ctx", None),
        P("fsdp", None, "ctx"),
    )
    out_specs = (P("fsdp", None, "ctx"), P("fsdp", "ctx", None), P("ctx", None))
    return jax.shard_map(body, mesh=mesh, in_specs=in_specs, out_specs=out_specs, check_vma=False)
```

```python
import math

import jax
import jax.numpy as jnp
from jax import lax
from jax.experimental import pallas as pl
from jax.experimental.pallas import tpu as pltpu
from jax.sharding import PartitionSpec as P

MESH = pl.DeviceIdType.MESH
BF = jnp.bfloat16
F32 = jnp.float32
FULL = slice(None)
SUBS = (0, 3, 1, 2)
ORDERS = ((0, 1, 2), (1, 2, 0), (2, 0, 1))


def my_coords():
    f = lax.axis_index("fsdp")
    t = lax.axis_index("ctx")
    return f % 2, (t // 8, (t // 2) % 4, (t % 2) * 2 + f // 2)


def device_of(core, pos):
    z, x, y = pos
    return ((y % 2) * 2 + core, z * 8 + x * 2 + y // 2)


def moved(pos, axis, by):
    out = list(pos)
    out[axis] = (pos[axis] + by) % 4
    return tuple(out)


def shards(ref, part, core, pos, half=None):
    z, x, y = pos
    rows = FULL if half is None else pl.ds(half * 32, 32)
    yl = FULL if y is None else y % 2
    yh = FULL if y is None else y // 2
    z = FULL if z is None else z
    x = FULL if x is None else x
    return ref.at[part, yl, core, z, x, yh, rows, :]


class Gather:
    def __init__(self, w, own, send, recv, sib_send, sib_recv):
        self.w, self.own = w, own
        self.send, self.recv = send, recv
        self.sib_send, self.sib_recv = sib_send, sib_recv
        self.core, self.pos = my_coords()
        self.started = []

    def block(self, part, phase, at, half=None, core=None, sub=None):
        order = ORDERS[part]
        pos = [None, None, None]
        for later in order[phase + 1 :]:
            pos[later] = self.pos[later]
        pos[order[phase]] = at
        if sub is not None:
            pos[order[1]] = (self.pos[order[1]] + sub) % 4
        return shards(self.w, part, self.core if core is None else core, pos, half)

    def copy(self, part, phase, kind, at, by, half=None, sub=None):
        axis = ORDERS[part][phase]
        ref = self.block(part, phase, at, half, sub=sub)
        at = (part, phase, kind) if sub is None else (part, 2 + sub, kind)
        return pltpu.make_async_remote_copy(
            src_ref=ref,
            dst_ref=ref,
            send_sem=self.send.at[at],
            recv_sem=self.recv.at[at],
            device_id=device_of(self.core, moved(self.pos, axis, by)),
            device_id_type=MESH,
        )

    def go(self, c):
        c.start()
        self.started.append(c)

    def me(self, part, phase):
        return self.pos[ORDERS[part][phase]]

    def first(self, part, phase, sub=None):
        m = self.me(part, phase)
        self.go(self.copy(part, phase, 0, m, 1, sub=sub))
        self.go(self.copy(part, phase, 1, m, -1, sub=sub))

    def forward(self, part, phase, kind, sub=None):
        m = self.me(part, phase)
        by = 1 if kind == 0 else -1
        at = (m - by) % 4
        self.copy(part, phase, kind, at, by, sub=sub).wait_recv()
        self.go(self.copy(part, phase, 2 + kind, at, by, half=kind, sub=sub))
        if phase == 2:
            self.go(self.sibling(part, 1 + kind, sub))

    def last(self, part, phase, kind, sub=None):
        m = self.me(part, phase)
        self.copy(part, phase, 2 + kind, (m + 2) % 4, 1, half=kind, sub=sub).wait_recv()
        if phase == 2:
            self.go(self.sibling(part, 3 + kind, sub))

    def sibling(self, part, kind, sub, receive=False):
        core = 1 - self.core if receive else self.core
        at = (self.me(part, 2) + (0, -1, 1, 2, 2)[kind]) % 4
        ref = self.block(part, 2, at, None if kind < 3 else kind - 3, core, sub)
        return pltpu.make_async_remote_copy(
            src_ref=ref,
            dst_ref=ref,
            send_sem=self.sib_send.at[part, sub, kind],
            recv_sem=self.sib_recv.at[part, sub, kind],
            device_id=device_of(1 - self.core, self.pos),
            device_id_type=MESH,
        )

    def from_sibling(self, part, kinds, subs):
        for sub in subs:
            for kind in kinds:
                self.sibling(part, kind, sub, receive=True).wait_recv()

    def wait_sends(self):
        for c in self.started:
            c.wait_send()


DN_NT = (((1,), (1,)), ((), ()))
KK = 8


def lanes(shape):
    return lax.broadcasted_iota(jnp.int32, shape, len(shape) - 1)


def fill_toeplitz(h_ref, s_ref):
    @pl.loop(0, 32, unroll=2)
    def _(k):
        now = h_ref[:, pl.ds(pl.multiple_of(256 * k, 256), 256)]
        earlier = jnp.maximum(k - 1, 0)
        before = h_ref[:, pl.ds(pl.multiple_of(256 * earlier, 256), 256)]
        before = jnp.where(k > 0, before, 0.0)
        row = jnp.concatenate([before, now], axis=1)
        base = pltpu.roll(jnp.broadcast_to(row, (8, 512)), 0, 1, stride=1, stride_axis=0)
        for b in range(8):
            one = base if b == 0 else pltpu.roll(base, 16 * b, 1)
            two = pltpu.roll(base, 16 * b + 8, 1)
            pair = jnp.concatenate([one, two], axis=0).astype(BF)
            s_ref[k, 16 * b : 16 * b + 16, :] = pair[:, 256:512]
            s_ref[k, 128 + 16 * b : 144 + 16 * b, :] = pair[:, 128:384]


def fill_taps(taps_ref, tap_ref, group):
    lane = lanes((16, 512))
    chan = lax.broadcasted_iota(jnp.int32, (16, 512), 0)
    pick = (lane == group * 16 + chan).astype(F32)
    for tap in range(3):
        for part in range(3):
            row = taps_ref[tap : tap + 1, 512 * part : 512 * part + 512]
            col = jnp.sum(pick * row, axis=1, keepdims=True)
            tap_ref[3 * tap + part] = jnp.broadcast_to(col, (16, 256))


def conv_front(x_ref, u_ref, tap_ref, wide_ref, mpad_ref, gpad_ref):
    lane = lanes((16, 256))
    mpad_ref[0:512, :] = jnp.zeros((512, 256), BF)
    gpad_ref[512:1024, :] = jnp.zeros((512, 256), BF)

    @pl.loop(0, 32, unroll=4)
    def _(a):
        prev = jnp.maximum(a - 1, 0)
        got = []
        for part in range(3):
            x = x_ref[part, a].astype(F32)
            y = x_ref[part, prev].astype(F32)
            y = jnp.where(a > 0, y, 0.0)
            one = jnp.where(lane < 1, pltpu.roll(y, 1, 1), pltpu.roll(x, 1, 1))
            two = jnp.where(lane < 2, pltpu.roll(y, 2, 1), pltpu.roll(x, 2, 1))
            short = tap_ref[part] * x + tap_ref[3 + part] * one + tap_ref[6 + part] * two
            wide_ref[part, a] = short
            got.append(short)
        rows = pl.ds(pl.multiple_of(16 * a, 16), 16)
        later = pl.ds(pl.multiple_of(512 + 16 * a, 16), 16)
        mpad_ref[later, :] = (got[1] * got[2]).astype(BF)
        gpad_ref[rows, :] = (u_ref[a].astype(F32) * got[0]).astype(BF)


def long_conv(mpad_ref, s_ref, acc_ref):
    for n in range(32 // KK):
        low = 16 * KK * n
        lhs = [mpad_ref[512 + low - 16 * k : 1024 - 16 * k, :] for k in range(n * KK, n * KK + KK)]
        rhs = s_ref[n * KK : n * KK + KK].reshape(256 * KK, 256)
        out = jnp.dot(jnp.concatenate(lhs, axis=1), rhs, preferred_element_type=F32)
        if n == 0:
            acc_ref[...] = out
        else:
            acc_ref[low:512, :] += out


def long_back(gpad_ref, s_ref, acc_ref):
    for n in range(32 // KK):
        high = 512 - 16 * KK * n
        lhs = [gpad_ref[16 * k : 16 * k + high, :] for k in range(n * KK, n * KK + KK)]
        rhs = [s_ref[k] for k in range(n * KK, n * KK + KK)]
        out = lax.dot_general(
            jnp.concatenate(lhs, axis=1), jnp.concatenate(rhs, axis=1), DN_NT, preferred_element_type=F32
        )
        if n == 0:
            acc_ref[...] = out
        else:
            acc_ref[0:high, :] += out


def gate_and_query_grad(acc_ref, u_ref, wide_ref, gated_ref, grad_ref):
    @pl.loop(0, 32, unroll=4)
    def _(a):
        rows = pl.ds(pl.multiple_of(16 * a, 16), 16)
        conv = acc_ref[rows, :].astype(BF).astype(F32)
        gated_ref[a] = (wide_ref[0, a] * conv).astype(BF)
        grad_ref[0, a] = u_ref[a].astype(F32) * conv


def back_taps(part, a, tap_ref, grad_ref, pg_ref):
    lane = lanes((16, 256))
    x = grad_ref[part, a]
    y = grad_ref[part, a + 1]
    one = jnp.where(lane > 254, pltpu.roll(y, 255, 1), pltpu.roll(x, 255, 1))
    two = jnp.where(lane > 253, pltpu.roll(y, 254, 1), pltpu.roll(x, 254, 1))
    out = tap_ref[part] * x + tap_ref[3 + part] * one + tap_ref[6 + part] * two
    pg_ref[part, a] = out.astype(BF)


def query_back(tap_ref, grad_ref, pg_ref):
    @pl.loop(0, 32, unroll=4)
    def _(a):
        back_taps(0, a, tap_ref, grad_ref, pg_ref)


def key_value_back(acc_ref, wide_ref, tap_ref, grad_ref, pg_ref):
    grad_ref[:, 32] = jnp.zeros((3, 16, 256), F32)

    @pl.loop(0, 32, unroll=4)
    def _(a):
        rows = pl.ds(pl.multiple_of(16 * a, 16), 16)
        mg = acc_ref[rows, :].astype(BF).astype(F32)
        grad_ref[1, a] = mg * wide_ref[2, a]
        grad_ref[2, a] = mg * wide_ref[1, a]

    @pl.loop(0, 32, unroll=4)
    def _(a):
        back_taps(1, a, tap_ref, grad_ref, pg_ref)
        back_taps(2, a, tap_ref, grad_ref, pg_ref)


def filter_back(mpad_ref, gpad_ref, mt_ref, z_ref, out_ref):
    mt_ref[...] = mpad_ref[512:1024, :].astype(F32).T.astype(BF)
    for n in range(32 // KK):
        deep = 512 - 16 * KK * n

        @pl.loop(n * KK // 4, n * KK // 4 + KK // 4)
        def _(m):
            four = [gpad_ref[pl.ds(pl.multiple_of(64 * m + 16 * i, 16), deep), :] for i in range(4)]
            wide = jnp.dot(mt_ref[:, 0:deep], jnp.concatenate(four, axis=1), preferred_element_type=F32)
            for i in range(4):
                q = wide[:, 256 * i : 256 * i + 256]
                top, low = q[0:128], q[128:256]
                mid = top[:, 0:128] + low[:, 128:256]
                blank = jnp.zeros((128, 128), F32)
                x = jnp.concatenate([blank, low[:, 0:128], mid, top[:, 128:256]], axis=1)
                for half in (64, 32, 16, 8):
                    x = x[0:half] + pltpu.roll(x[half : 2 * half], 512 - half, 1)
                z_ref[4 * m + i] = x

    for k in range(32):
        x = z_ref[k, :, 256:512]
        y = z_ref[k + 1, :, 0:256] if k < 31 else jnp.zeros((8, 256), F32)
        after = z_ref[k + 1, :, 256:512] if k < 31 else jnp.zeros((8, 256), F32)
        if k < 30:
            after += z_ref[k + 2, :, 0:256]
        x = jnp.concatenate([x + y, after], axis=1)
        row = lax.broadcasted_iota(jnp.int32, x.shape, 0)
        for bit in (1, 2, 4):
            x = jnp.where(row // bit % 2 == 1, pltpu.roll(x, 512 - bit, 1), x)
        out_ref[:, 256 * k : 256 * k + 256] = jnp.sum(x[:, 0:256], axis=0, keepdims=True)


def each_peer(step, unroll=1):
    @pl.loop(1, 32, unroll=unroll)
    def _(d):
        step(d)


class Exchange:
    def __init__(self, src, dst, send, recv):
        self.src, self.dst, self.send, self.recv = src, dst, send, recv
        self.f, self.t = lax.axis_index("fsdp"), lax.axis_index("ctx")

    def copy(self, d):
        peer = (self.t + d) % 32
        return pltpu.make_async_remote_copy(
            src_ref=self.src(peer),
            dst_ref=self.dst(self.t),
            send_sem=self.send.at[d],
            recv_sem=self.recv.at[d],
            device_id=(self.f, peer),
            device_id_type=MESH,
        )

    def start(self):
        each_peer(lambda d: self.copy(d).start(), 31)

    def wait_recv(self):
        each_peer(lambda d: self.copy(d).wait_recv())

    def wait_send(self):
        each_peer(lambda d: self.copy(d).wait_send())


def project(part, near, subs, pos, tok, w, acc):
    z, x, y = pos
    left, right = [], []

    def piece(row, size, block):
        left.append(tok[:, pl.ds(pl.multiple_of(row * size, size), size)])
        right.append(block.reshape(size, 512))

    for fc in range(2):
        if part == 0:
            fy = (y + near) % 2
            for sub in subs:
                fx = (x + sub) % 4
                for fz in range(4):
                    piece(((fy * 2 + fc) * 4 + fz) * 4 + fx, 128, w[part, fy, fc, fz, fx])
        for hop in (0, 2):
            if part == 1:
                fz = (z + near + hop) % 4
                for sub in subs:
                    if sub < 2:
                        fy = (y + sub) % 2
                        piece((fy * 2 + fc) * 4 + fz, 512, w[part, fy, fc, fz])
            if part == 2:
                fx = (x + near + hop) % 4
                for fy in range(2):
                    for sub in subs:
                        fz = (z + sub) % 4
                        piece(((fy * 2 + fc) * 4 + fz) * 4 + fx, 128, w[part, fy, fc, fz, fx])
    acc[part] += jnp.dot(
        jnp.concatenate(left, axis=1), jnp.concatenate(right, axis=0), preferred_element_type=F32
    )


def kernel(
    tok_hbm, own, taps, h, cot_hbm,
    gated_out, grad_out, filter_out,
    w, tok, acc3, p, x, u, s, tap, wide, mpad, gpad, acc, grad, pg, r, mt, z8, gated, fmine, fgot,
    put, send, recv, sib_send, sib_recv, local, a2a_send, a2a_recv, f_send, f_recv, out_sem,
):
    g = Gather(w, own, send, recv, sib_send, sib_recv)
    f, t = lax.axis_index("fsdp"), lax.axis_index("ctx")
    core, pos = g.core, g.pos
    barrier = pltpu.get_barrier_semaphore()

    def hello(device):
        pl.semaphore_signal(barrier, inc=1, device_id=device, device_id_type=MESH)

    for axis in range(3):
        for by in (1, -1):
            hello(device_of(core, moved(pos, axis, by)))
    hello(device_of(1 - core, pos))
    load = pltpu.make_async_copy(tok_hbm, tok, local.at[0])
    load.start()
    mine = []
    for part in range(3):
        c = pltpu.make_async_copy(
            own.at[:, pl.ds(512 * part, 512)], shards(w, part, core, pos), put.at[part]
        )
        c.start()
        mine.append(c)
    my_cot = pltpu.make_async_copy(cot_hbm.at[t], u.at[t], local.at[1])
    my_cot.start()
    for c in mine:
        c.wait()
    pl.semaphore_wait(barrier, 7)

    cots = Exchange(lambda q: cot_hbm.at[q], lambda q: u.at[q], a2a_send.at[0], a2a_recv.at[0])
    projs = Exchange(lambda q: p.at[:, q], lambda q: x.at[:, q], a2a_send.at[1], a2a_recv.at[1])
    gates = Exchange(lambda q: gated.at[q], lambda q: gated_out.at[q], a2a_send.at[2], a2a_recv.at[2])
    firsts = Exchange(lambda q: pg.at[0, q], lambda q: r.at[0, q], a2a_send.at[3], a2a_recv.at[3])
    others = Exchange(
        lambda q: pg.at[pl.ds(1, 2), q], lambda q: r.at[pl.ds(1, 2), q], a2a_send.at[4], a2a_recv.at[4]
    )

    parts = range(3)
    for part in parts:
        g.first(part, 0)
    fill_taps(taps, tap, t)
    acc3[...] = jnp.zeros_like(acc3)
    for kind in range(2):
        for part in parts:
            g.forward(part, 0, kind)
    for part in parts:
        for kind in range(2):
            g.last(part, 0, kind)
        g.first(part, 1)
        g.first(part, 2, 0)
        g.go(g.sibling(part, 0, 0))
    fill_toeplitz(h, s)
    for kind in range(2):
        for part in parts:
            g.forward(part, 1, kind)
            g.first(part, 2, SUBS[1 + kind])
            g.go(g.sibling(part, 0, SUBS[1 + kind]))
    for part in parts:
        for kind in range(2):
            g.last(part, 1, kind)
        g.first(part, 2, 2)
        g.go(g.sibling(part, 0, 2))
    load.wait()

    def forwards(sub):
        for kind in range(2):
            for part in parts:
                g.forward(part, 2, kind, sub)

    def lasts(sub):
        for part in parts:
            for kind in range(2):
                g.last(part, 2, kind, sub)

    def add(near, part, subs):
        for sub in subs:
            g.from_sibling(part, (1, 2) if near else (0, 3, 4), (sub,))
        project(part, near, subs, pos, tok, w, acc3)

    forwards(0)
    forwards(3)
    add(1, 0, (0,))
    add(1, 2, (0,))
    forwards(1)
    add(1, 0, (3,))
    add(1, 2, (3,))
    add(1, 1, (3, 1))
    forwards(2)
    lasts(0)
    add(1, 0, (1, 2))
    add(1, 2, (1, 2))
    lasts(3)
    add(1, 1, (0, 2))
    add(0, 0, (0, 3))
    lasts(1)
    add(0, 2, (0, 3))
    add(0, 1, (3, 1))
    add(0, 0, (1,))
    add(0, 2, (1,))
    lasts(2)
    cots.start()
    for part, subs in ((0, (2,)), (2, (2,)), (1, (0, 2))):
        add(0, part, subs)
        p[part] = acc3[part].T.astype(BF).reshape(32, 16, 256)
    projs.start()
    for part in range(3):
        x[part, t] = p[part, t]
    my_cot.wait()
    cots.wait_recv()
    projs.wait_recv()

    conv_front(x, u, tap, wide, mpad, gpad)
    long_back(gpad, s, acc)
    key_value_back(acc, wide, tap, grad, pg)
    others.start()
    for part in (1, 2):
        r[part, t] = pg[part, t]
    long_conv(mpad, s, acc)
    gate_and_query_grad(acc, u, wide, gated, grad)
    query_back(tap, grad, pg)
    firsts.start()
    r[0, t] = pg[0, t]
    gates.start()
    my_gate = pltpu.make_async_copy(gated.at[t], gated_out.at[t], local.at[2])
    my_gate.start()

    filter_back(mpad, gpad, mt, z8, fmine)
    shares = []
    for d in range(1, 4):
        c = pltpu.make_async_remote_copy(
            src_ref=fmine,
            dst_ref=fgot.at[d],
            send_sem=f_send.at[d],
            recv_sem=f_recv.at[d],
            device_id=((f + d) % 4, t),
            device_id_type=MESH,
        )
        c.start()
        shares.append(c)

    def weights(part, n):
        return w[part, n // 4, n // 2 % 2, pl.ds(n % 2 * 2, 2)].reshape(1024, 512)

    others.wait_recv()
    firsts.wait_recv()

    def store(n):
        at = pl.ds(pl.multiple_of(1024 * n, 1024), 1024)
        return pltpu.make_async_copy(tok.at[:, at], grad_out.at[:, at], out_sem.at[n])

    @pl.loop(0, 8)
    def _(n):
        lhs = jnp.concatenate([weights(part, n) for part in parts], axis=1)
        out = jnp.dot(lhs, r[...].reshape(1536, 256), preferred_element_type=F32)
        tok[:, pl.ds(pl.multiple_of(1024 * n, 1024), 1024)] = out.astype(BF).T
        store(n).start()

    for c in shares:
        c.wait_recv()
    scale = 1.0 / math.sqrt(4 * 16 * 8192)
    filter_out[...] = ((fmine[...] + fgot[1]) + (fgot[2] + fgot[3])) * scale
    my_gate.wait()
    gates.wait_recv()
    for e in (cots, projs, gates, firsts, others):
        e.wait_send()
    for c in shares:
        c.wait_send()
    g.wait_sends()

    @pl.loop(0, 8)
    def _(n):
        store(n).wait()


def body(tokens, projection, short_taps, long_filters, cotangent):
    vmem = pl.BlockSpec(memory_space=pltpu.VMEM)
    hbm = pl.BlockSpec(memory_space=pl.ANY)
    dma = pltpu.SemaphoreType.DMA
    gated, token_grad, filter_grad = pl.pallas_call(
        kernel,
        out_shape=[
            jax.ShapeDtypeStruct((32, 16, 256), BF),
            jax.ShapeDtypeStruct((256, 8192), BF),
            jax.ShapeDtypeStruct((1, 8192), F32),
        ],
        in_specs=[hbm, vmem, vmem, vmem, hbm],
        out_specs=[hbm, hbm, vmem],
        scratch_shapes=[
            pltpu.VMEM((3, 2, 2, 4, 4, 2, 64, 512), BF),
            pltpu.VMEM((256, 8192), BF),
            pltpu.VMEM((3, 256, 512), F32),
            pltpu.VMEM((3, 32, 16, 256), BF),
            pltpu.VMEM((3, 32, 16, 256), BF),
            pltpu.VMEM((32, 16, 256), BF),
            pltpu.VMEM((32, 256, 256), BF),
            pltpu.VMEM((9, 16, 256), F32),
            pltpu.VMEM((3, 32, 16, 256), F32),
            pltpu.VMEM((1024, 256), BF),
            pltpu.VMEM((1024, 256), BF),
            pltpu.VMEM((512, 256), F32),
            pltpu.VMEM((3, 33, 16, 256), F32),
            pltpu.VMEM((3, 32, 16, 256), BF),
            pltpu.VMEM((3, 32, 16, 256), BF),
            pltpu.VMEM((256, 512), BF),
            pltpu.VMEM((32, 8, 512), F32),
            pltpu.VMEM((32, 16, 256), BF),
            pltpu.VMEM((1, 8192), F32),
            pltpu.VMEM((4, 1, 8192), F32),
            dma((3,)),
            dma((3, 6, 4)),
            dma((3, 6, 4)),
            dma((3, 4, 5)),
            dma((3, 4, 5)),
            dma((3,)),
            dma((5, 32)),
            dma((5, 32)),
            dma((4,)),
            dma((4,)),
            dma((8,)),
        ],
        compiler_params=pltpu.CompilerParams(
            collective_id=0, has_side_effects=True, vmem_limit_bytes=46 * 1024 * 1024
        ),
    )(tokens[0], projection, short_taps, long_filters, cotangent[0].reshape(32, 16, 256))
    return gated.reshape(1, 512, 256), token_grad[None], filter_grad


def solution(mesh):
    in_specs = (
        P("fsdp", "ctx", None),
        P(("fsdp", "ctx"), None),
        P(),
        P("ctx", None),
        P("fsdp", None, "ctx"),
    )
    out_specs = (P("fsdp", None, "ctx"), P("fsdp", "ctx", None), P("ctx", None))
    return jax.shard_map(body, mesh=mesh, in_specs=in_specs, out_specs=out_specs, check_vma=False)
```

```python
import math

import jax
import jax.numpy as jnp
from jax import lax
from jax.experimental import pallas as pl
from jax.experimental.pallas import tpu as pltpu
from jax.sharding import PartitionSpec as P

MESH = pl.DeviceIdType.MESH
BF = jnp.bfloat16
F32 = jnp.float32
FULL = slice(None)
SUBS = (0, 3, 1, 2)
ORDERS = ((0, 1, 2), (1, 2, 0), (2, 0, 1))


def my_coords():
    f = lax.axis_index("fsdp")
    t = lax.axis_index("ctx")
    return f % 2, (t // 8, (t // 2) % 4, (t % 2) * 2 + f // 2)


def device_of(core, pos):
    z, x, y = pos
    return ((y % 2) * 2 + core, z * 8 + x * 2 + y // 2)


def moved(pos, axis, by):
    out = list(pos)
    out[axis] = (pos[axis] + by) % 4
    return tuple(out)


def shards(ref, part, core, pos, half=None):
    z, x, y = pos
    rows = FULL if half is None else pl.ds(half * 32, 32)
    yl = FULL if y is None else y % 2
    yh = FULL if y is None else y // 2
    z = FULL if z is None else z
    x = FULL if x is None else x
    return ref.at[part, yl, core, z, x, yh, rows, :]


class Gather:
    def __init__(self, w, own, send, recv, sib_send, sib_recv):
        self.w, self.own = w, own
        self.send, self.recv = send, recv
        self.sib_send, self.sib_recv = sib_send, sib_recv
        self.core, self.pos = my_coords()
        self.started = []

    def block(self, part, phase, at, half=None, core=None, sub=None):
        order = ORDERS[part]
        pos = [None, None, None]
        for later in order[phase + 1 :]:
            pos[later] = self.pos[later]
        pos[order[phase]] = at
        if sub is not None:
            pos[order[1]] = (self.pos[order[1]] + sub) % 4
        return shards(self.w, part, self.core if core is None else core, pos, half)

    def copy(self, part, phase, kind, at, by, half=None, sub=None):
        axis = ORDERS[part][phase]
        ref = self.block(part, phase, at, half, sub=sub)
        at = (part, phase, kind) if sub is None else (part, 2 + sub, kind)
        return pltpu.make_async_remote_copy(
            src_ref=ref,
            dst_ref=ref,
            send_sem=self.send.at[at],
            recv_sem=self.recv.at[at],
            device_id=device_of(self.core, moved(self.pos, axis, by)),
            device_id_type=MESH,
        )

    def go(self, c):
        c.start()
        self.started.append(c)

    def me(self, part, phase):
        return self.pos[ORDERS[part][phase]]

    def first(self, part, phase, sub=None):
        m = self.me(part, phase)
        self.go(self.copy(part, phase, 0, m, 1, sub=sub))
        self.go(self.copy(part, phase, 1, m, -1, sub=sub))

    def forward(self, part, phase, kind, sub=None):
        m = self.me(part, phase)
        by = 1 if kind == 0 else -1
        at = (m - by) % 4
        self.copy(part, phase, kind, at, by, sub=sub).wait_recv()
        self.go(self.copy(part, phase, 2 + kind, at, by, half=kind, sub=sub))
        if phase == 2:
            self.go(self.sibling(part, 1 + kind, sub))

    def last(self, part, phase, kind, sub=None):
        m = self.me(part, phase)
        self.copy(part, phase, 2 + kind, (m + 2) % 4, 1, half=kind, sub=sub).wait_recv()
        if phase == 2:
            self.go(self.sibling(part, 3 + kind, sub))

    def sibling(self, part, kind, sub, receive=False):
        core = 1 - self.core if receive else self.core
        at = (self.me(part, 2) + (0, -1, 1, 2, 2)[kind]) % 4
        ref = self.block(part, 2, at, None if kind < 3 else kind - 3, core, sub)
        return pltpu.make_async_remote_copy(
            src_ref=ref,
            dst_ref=ref,
            send_sem=self.sib_send.at[part, sub, kind],
            recv_sem=self.sib_recv.at[part, sub, kind],
            device_id=device_of(1 - self.core, self.pos),
            device_id_type=MESH,
        )

    def from_sibling(self, part, kinds, subs):
        for sub in subs:
            for kind in kinds:
                self.sibling(part, kind, sub, receive=True).wait_recv()

    def wait_sends(self):
        for c in self.started:
            c.wait_send()


DN_NT = (((1,), (1,)), ((), ()))
KK = 8


def lanes(shape):
    return lax.broadcasted_iota(jnp.int32, shape, len(shape) - 1)


def fill_toeplitz(h_ref, s_ref):
    @pl.loop(0, 32, unroll=2)
    def _(k):
        now = h_ref[:, pl.ds(pl.multiple_of(256 * k, 256), 256)]
        earlier = jnp.maximum(k - 1, 0)
        before = h_ref[:, pl.ds(pl.multiple_of(256 * earlier, 256), 256)]
        before = jnp.where(k > 0, before, 0.0)
        row = jnp.concatenate([before, now], axis=1)
        base = pltpu.roll(jnp.broadcast_to(row, (8, 512)), 0, 1, stride=1, stride_axis=0)
        for b in range(8):
            one = base if b == 0 else pltpu.roll(base, 16 * b, 1)
            two = pltpu.roll(base, 16 * b + 8, 1)
            pair = jnp.concatenate([one, two], axis=0).astype(BF)
            s_ref[k, 16 * b : 16 * b + 16, :] = pair[:, 256:512]
            s_ref[k, 128 + 16 * b : 144 + 16 * b, :] = pair[:, 128:384]


def fill_taps(taps_ref, tap_ref, group):
    lane = lanes((16, 512))
    chan = lax.broadcasted_iota(jnp.int32, (16, 512), 0)
    pick = (lane == group * 16 + chan).astype(F32)
    for tap in range(3):
        for part in range(3):
            row = taps_ref[tap : tap + 1, 512 * part : 512 * part + 512]
            col = jnp.sum(pick * row, axis=1, keepdims=True)
            tap_ref[3 * tap + part] = jnp.broadcast_to(col, (16, 256))


def conv_front(x_ref, u_ref, tap_ref, wide_ref, mpad_ref, gpad_ref):
    lane = lanes((16, 256))
    mpad_ref[0:512, :] = jnp.zeros((512, 256), BF)
    gpad_ref[512:1024, :] = jnp.zeros((512, 256), BF)

    @pl.loop(0, 32, unroll=4)
    def _(a):
        prev = jnp.maximum(a - 1, 0)
        got = []
        for part in range(3):
            x = x_ref[part, a].astype(F32)
            y = x_ref[part, prev].astype(F32)
            y = jnp.where(a > 0, y, 0.0)
            one = jnp.where(lane < 1, pltpu.roll(y, 1, 1), pltpu.roll(x, 1, 1))
            two = jnp.where(lane < 2, pltpu.roll(y, 2, 1), pltpu.roll(x, 2, 1))
            short = tap_ref[part] * x + tap_ref[3 + part] * one + tap_ref[6 + part] * two
            wide_ref[part, a] = short
            got.append(short)
        rows = pl.ds(pl.multiple_of(16 * a, 16), 16)
        later = pl.ds(pl.multiple_of(512 + 16 * a, 16), 16)
        mpad_ref[later, :] = (got[1] * got[2]).astype(BF)
        gpad_ref[rows, :] = (u_ref[a].astype(F32) * got[0]).astype(BF)


def long_conv(mpad_ref, s_ref, acc_ref):
    for n in range(32 // KK):
        low = 16 * KK * n
        lhs = [mpad_ref[512 + low - 16 * k : 1024 - 16 * k, :] for k in range(n * KK, n * KK + KK)]
        rhs = s_ref[n * KK : n * KK + KK].reshape(256 * KK, 256)
        out = jnp.dot(jnp.concatenate(lhs, axis=1), rhs, preferred_element_type=F32)
        if n == 0:
            acc_ref[...] = out
        else:
            acc_ref[low:512, :] += out


def long_back(gpad_ref, s_ref, acc_ref):
    for n in range(32 // KK):
        high = 512 - 16 * KK * n
        lhs = [gpad_ref[16 * k : 16 * k + high, :] for k in range(n * KK, n * KK + KK)]
        rhs = [s_ref[k] for k in range(n * KK, n * KK + KK)]
        out = lax.dot_general(
            jnp.concatenate(lhs, axis=1), jnp.concatenate(rhs, axis=1), DN_NT, preferred_element_type=F32
        )
        if n == 0:
            acc_ref[...] = out
        else:
            acc_ref[0:high, :] += out


def gate_and_query_grad(acc_ref, u_ref, wide_ref, gated_ref, grad_ref):
    @pl.loop(0, 32, unroll=4)
    def _(a):
        rows = pl.ds(pl.multiple_of(16 * a, 16), 16)
        conv = acc_ref[rows, :].astype(BF).astype(F32)
        gated_ref[a] = (wide_ref[0, a] * conv).astype(BF)
        grad_ref[0, a] = u_ref[a].astype(F32) * conv


def back_taps(part, a, tap_ref, grad_ref, pg_ref):
    lane = lanes((16, 256))
    x = grad_ref[part, a]
    y = grad_ref[part, a + 1]
    one = jnp.where(lane > 254, pltpu.roll(y, 255, 1), pltpu.roll(x, 255, 1))
    two = jnp.where(lane > 253, pltpu.roll(y, 254, 1), pltpu.roll(x, 254, 1))
    out = tap_ref[part] * x + tap_ref[3 + part] * one + tap_ref[6 + part] * two
    pg_ref[part, a] = out.astype(BF)


def query_back(tap_ref, grad_ref, pg_ref):
    @pl.loop(0, 32, unroll=4)
    def _(a):
        back_taps(0, a, tap_ref, grad_ref, pg_ref)


def key_value_back(acc_ref, wide_ref, tap_ref, grad_ref, pg_ref):
    grad_ref[:, 32] = jnp.zeros((3, 16, 256), F32)

    @pl.loop(0, 32, unroll=4)
    def _(a):
        rows = pl.ds(pl.multiple_of(16 * a, 16), 16)
        mg = acc_ref[rows, :].astype(BF).astype(F32)
        grad_ref[1, a] = mg * wide_ref[2, a]
        grad_ref[2, a] = mg * wide_ref[1, a]

    @pl.loop(0, 32, unroll=4)
    def _(a):
        back_taps(1, a, tap_ref, grad_ref, pg_ref)
        back_taps(2, a, tap_ref, grad_ref, pg_ref)


def filter_back(mpad_ref, gpad_ref, mt_ref, z_ref, out_ref):
    mt_ref[...] = mpad_ref[512:1024, :].astype(F32).T.astype(BF)
    for n in range(32 // KK):
        deep = 512 - 16 * KK * n

        @pl.loop(n * KK // 4, n * KK // 4 + KK // 4)
        def _(m):
            four = [gpad_ref[pl.ds(pl.multiple_of(64 * m + 16 * i, 16), deep), :] for i in range(4)]
            wide = jnp.dot(mt_ref[:, 0:deep], jnp.concatenate(four, axis=1), preferred_element_type=F32)
            for i in range(4):
                q = wide[:, 256 * i : 256 * i + 256]
                top, low = q[0:128], q[128:256]
                mid = top[:, 0:128] + low[:, 128:256]
                blank = jnp.zeros((128, 128), F32)
                x = jnp.concatenate([blank, low[:, 0:128], mid, top[:, 128:256]], axis=1)
                for half in (64, 32, 16, 8):
                    x = x[0:half] + pltpu.roll(x[half : 2 * half], 512 - half, 1)
                z_ref[4 * m + i] = x

    for k in range(32):
        x = z_ref[k, :, 256:512]
        y = z_ref[k + 1, :, 0:256] if k < 31 else jnp.zeros((8, 256), F32)
        after = z_ref[k + 1, :, 256:512] if k < 31 else jnp.zeros((8, 256), F32)
        if k < 30:
            after += z_ref[k + 2, :, 0:256]
        x = jnp.concatenate([x + y, after], axis=1)
        row = lax.broadcasted_iota(jnp.int32, x.shape, 0)
        for bit in (1, 2, 4):
            x = jnp.where(row // bit % 2 == 1, pltpu.roll(x, 512 - bit, 1), x)
        out_ref[:, 256 * k : 256 * k + 256] = jnp.sum(x[:, 0:256], axis=0, keepdims=True)


def each_peer(step, unroll=1):
    @pl.loop(1, 32, unroll=unroll)
    def _(d):
        step(d)


class Exchange:
    def __init__(self, src, dst, send, recv):
        self.src, self.dst, self.send, self.recv = src, dst, send, recv
        self.f, self.t = lax.axis_index("fsdp"), lax.axis_index("ctx")

    def copy(self, d):
        peer = (self.t + d) % 32
        return pltpu.make_async_remote_copy(
            src_ref=self.src(peer),
            dst_ref=self.dst(self.t),
            send_sem=self.send.at[d],
            recv_sem=self.recv.at[d],
            device_id=(self.f, peer),
            device_id_type=MESH,
        )

    def start(self):
        each_peer(lambda d: self.copy(d).start(), 31)

    def wait_recv(self):
        each_peer(lambda d: self.copy(d).wait_recv(), 31)

    def wait_send(self):
        each_peer(lambda d: self.copy(d).wait_send(), 31)


def project(part, near, subs, pos, tok, w, acc):
    z, x, y = pos
    left, right = [], []

    def piece(row, size, block):
        left.append(tok[:, pl.ds(pl.multiple_of(row * size, size), size)])
        right.append(block.reshape(size, 512))

    for fc in range(2):
        if part == 0:
            fy = (y + near) % 2
            for sub in subs:
                fx = (x + sub) % 4
                for fz in range(4):
                    piece(((fy * 2 + fc) * 4 + fz) * 4 + fx, 128, w[part, fy, fc, fz, fx])
        for hop in (0, 2):
            if part == 1:
                fz = (z + near + hop) % 4
                for sub in subs:
                    if sub < 2:
                        fy = (y + sub) % 2
                        piece((fy * 2 + fc) * 4 + fz, 512, w[part, fy, fc, fz])
            if part == 2:
                fx = (x + near + hop) % 4
                for fy in range(2):
                    for sub in subs:
                        fz = (z + sub) % 4
                        piece(((fy * 2 + fc) * 4 + fz) * 4 + fx, 128, w[part, fy, fc, fz, fx])
    acc[part] += jnp.dot(
        jnp.concatenate(left, axis=1), jnp.concatenate(right, axis=0), preferred_element_type=F32
    )


def kernel(
    tok_hbm, own, taps, h, cot_hbm,
    gated_out, grad_out, filter_out,
    w, tok, acc3, p, x, u, s, tap, wide, mpad, gpad, acc, grad, pg, r, mt, z8, gated, fmine, fgot,
    put, send, recv, sib_send, sib_recv, local, a2a_send, a2a_recv, f_send, f_recv, out_sem,
):
    g = Gather(w, own, send, recv, sib_send, sib_recv)
    f, t = lax.axis_index("fsdp"), lax.axis_index("ctx")
    core, pos = g.core, g.pos
    barrier = pltpu.get_barrier_semaphore()

    def hello(device):
        pl.semaphore_signal(barrier, inc=1, device_id=device, device_id_type=MESH)

    for axis in range(3):
        for by in (1, -1):
            hello(device_of(core, moved(pos, axis, by)))
    hello(device_of(1 - core, pos))
    load = pltpu.make_async_copy(tok_hbm, tok, local.at[0])
    load.start()
    mine = []
    for part in range(3):
        c = pltpu.make_async_copy(
            own.at[:, pl.ds(512 * part, 512)], shards(w, part, core, pos), put.at[part]
        )
        c.start()
        mine.append(c)
    my_cot = pltpu.make_async_copy(cot_hbm.at[t], u.at[t], local.at[1])
    my_cot.start()
    for c in mine:
        c.wait()
    pl.semaphore_wait(barrier, 7)

    cots = Exchange(lambda q: cot_hbm.at[q], lambda q: u.at[q], a2a_send.at[0], a2a_recv.at[0])
    projs = Exchange(lambda q: p.at[:, q], lambda q: x.at[:, q], a2a_send.at[1], a2a_recv.at[1])
    gates = Exchange(lambda q: gated.at[q], lambda q: gated_out.at[q], a2a_send.at[2], a2a_recv.at[2])
    firsts = Exchange(lambda q: pg.at[0, q], lambda q: r.at[0, q], a2a_send.at[3], a2a_recv.at[3])
    others = Exchange(
        lambda q: pg.at[pl.ds(1, 2), q], lambda q: r.at[pl.ds(1, 2), q], a2a_send.at[4], a2a_recv.at[4]
    )

    parts = range(3)
    for part in parts:
        g.first(part, 0)
    fill_taps(taps, tap, t)
    acc3[...] = jnp.zeros_like(acc3)
    for kind in range(2):
        for part in parts:
            g.forward(part, 0, kind)
    for part in parts:
        for kind in range(2):
            g.last(part, 0, kind)
        g.first(part, 1)
        g.first(part, 2, 0)
        g.go(g.sibling(part, 0, 0))
    fill_toeplitz(h, s)
    for kind in range(2):
        for part in parts:
            g.forward(part, 1, kind)
            g.first(part, 2, SUBS[1 + kind])
            g.go(g.sibling(part, 0, SUBS[1 + kind]))
    for part in parts:
        for kind in range(2):
            g.last(part, 1, kind)
        g.first(part, 2, 2)
        g.go(g.sibling(part, 0, 2))
    load.wait()

    def forwards(sub):
        for kind in range(2):
            for part in parts:
                g.forward(part, 2, kind, sub)

    def lasts(sub):
        for part in parts:
            for kind in range(2):
                g.last(part, 2, kind, sub)

    def add(near, part, subs):
        for sub in subs:
            g.from_sibling(part, (1, 2) if near else (0, 3, 4), (sub,))
        project(part, near, subs, pos, tok, w, acc3)

    forwards(0)
    forwards(3)
    add(1, 0, (0,))
    add(1, 2, (0,))
    forwards(1)
    add(1, 0, (3,))
    add(1, 2, (3,))
    add(1, 1, (3, 1))
    forwards(2)
    lasts(0)
    add(1, 0, (1, 2))
    add(1, 2, (1, 2))
    lasts(3)
    add(1, 1, (0, 2))
    add(0, 0, (0, 3))
    lasts(1)
    add(0, 2, (0, 3))
    add(0, 1, (3, 1))
    add(0, 0, (1,))
    add(0, 2, (1,))
    lasts(2)
    cots.start()
    for part, subs in ((0, (2,)), (2, (2,)), (1, (0, 2))):
        add(0, part, subs)
        p[part] = acc3[part].T.astype(BF).reshape(32, 16, 256)
    projs.start()
    for part in range(3):
        x[part, t] = p[part, t]
    my_cot.wait()
    g.wait_sends()
    cots.wait_recv()
    cots.wait_send()
    projs.wait_recv()

    conv_front(x, u, tap, wide, mpad, gpad)
    long_back(gpad, s, acc)
    key_value_back(acc, wide, tap, grad, pg)
    others.start()
    for part in (1, 2):
        r[part, t] = pg[part, t]
    long_conv(mpad, s, acc)
    gate_and_query_grad(acc, u, wide, gated, grad)
    query_back(tap, grad, pg)
    firsts.start()
    r[0, t] = pg[0, t]

    filter_back(mpad, gpad, mt, z8, fmine)
    shares = []
    for d in range(1, 4):
        c = pltpu.make_async_remote_copy(
            src_ref=fmine,
            dst_ref=fgot.at[d],
            send_sem=f_send.at[d],
            recv_sem=f_recv.at[d],
            device_id=((f + d) % 4, t),
            device_id_type=MESH,
        )
        c.start()
        shares.append(c)

    def weights(part, n):
        return w[part, n // 4, n // 2 % 2, pl.ds(n % 2 * 2, 2)].reshape(1024, 512)

    gates.start()
    my_gate = pltpu.make_async_copy(gated.at[t], gated_out.at[t], local.at[2])
    my_gate.start()
    projs.wait_send()
    others.wait_recv()
    firsts.wait_recv()

    def store(n):
        at = pl.ds(pl.multiple_of(1024 * n, 1024), 1024)
        return pltpu.make_async_copy(tok.at[:, at], grad_out.at[:, at], out_sem.at[n])

    @pl.loop(0, 8)
    def _(n):
        lhs = jnp.concatenate([weights(part, n) for part in parts], axis=1)
        out = jnp.dot(lhs, r[...].reshape(1536, 256), preferred_element_type=F32)
        tok[:, pl.ds(pl.multiple_of(1024 * n, 1024), 1024)] = out.astype(BF).T
        store(n).start()

    for c in shares:
        c.wait_recv()
    scale = 1.0 / math.sqrt(4 * 16 * 8192)
    filter_out[...] = ((fmine[...] + fgot[1]) + (fgot[2] + fgot[3])) * scale
    my_gate.wait()
    gates.wait_recv()
    for e in (gates, firsts, others):
        e.wait_send()
    for c in shares:
        c.wait_send()

    @pl.loop(0, 8)
    def _(n):
        store(n).wait()


def body(tokens, projection, short_taps, long_filters, cotangent):
    vmem = pl.BlockSpec(memory_space=pltpu.VMEM)
    hbm = pl.BlockSpec(memory_space=pl.ANY)
    dma = pltpu.SemaphoreType.DMA
    gated, token_grad, filter_grad = pl.pallas_call(
        kernel,
        out_shape=[
            jax.ShapeDtypeStruct((32, 16, 256), BF),
            jax.ShapeDtypeStruct((256, 8192), BF),
            jax.ShapeDtypeStruct((1, 8192), F32),
        ],
        in_specs=[hbm, vmem, vmem, vmem, hbm],
        out_specs=[hbm, hbm, vmem],
        scratch_shapes=[
            pltpu.VMEM((3, 2, 2, 4, 4, 2, 64, 512), BF),
            pltpu.VMEM((256, 8192), BF),
            pltpu.VMEM((3, 256, 512), F32),
            pltpu.VMEM((3, 32, 16, 256), BF),
            pltpu.VMEM((3, 32, 16, 256), BF),
            pltpu.VMEM((32, 16, 256), BF),
            pltpu.VMEM((32, 256, 256), BF),
            pltpu.VMEM((9, 16, 256), F32),
            pltpu.VMEM((3, 32, 16, 256), F32),
            pltpu.VMEM((1024, 256), BF),
            pltpu.VMEM((1024, 256), BF),
            pltpu.VMEM((512, 256), F32),
            pltpu.VMEM((3, 33, 16, 256), F32),
            pltpu.VMEM((3, 32, 16, 256), BF),
            pltpu.VMEM((3, 32, 16, 256), BF),
            pltpu.VMEM((256, 512), BF),
            pltpu.VMEM((32, 8, 512), F32),
            pltpu.VMEM((32, 16, 256), BF),
            pltpu.VMEM((1, 8192), F32),
            pltpu.VMEM((4, 1, 8192), F32),
            dma((3,)),
            dma((3, 6, 4)),
            dma((3, 6, 4)),
            dma((3, 4, 5)),
            dma((3, 4, 5)),
            dma((3,)),
            dma((5, 32)),
            dma((5, 32)),
            dma((4,)),
            dma((4,)),
            dma((8,)),
        ],
        compiler_params=pltpu.CompilerParams(
            collective_id=0, has_side_effects=True, vmem_limit_bytes=46 * 1024 * 1024
        ),
    )(tokens[0], projection, short_taps, long_filters, cotangent[0].reshape(32, 16, 256))
    return gated.reshape(1, 512, 256), token_grad[None], filter_grad


def solution(mesh):
    in_specs = (
        P("fsdp", "ctx", None),
        P(("fsdp", "ctx"), None),
        P(),
        P("ctx", None),
        P("fsdp", None, "ctx"),
    )
    out_specs = (P("fsdp", None, "ctx"), P("fsdp", "ctx", None), P("ctx", None))
    return jax.shard_map(body, mesh=mesh, in_specs=in_specs, out_specs=out_specs, check_vma=False)
```
